32 devices in a mesh: blk: 8 (over y, x, core), rep: 4 (over z).
Axes of the slice: x: 2, y: 2, z: 4, core: 2. Of those that a mesh axis runs over, the one named last changes fastest.
Arguments:
- generated: float32 [2048, 1024], P(('blk', 'rep')), may hold values from -6 to 6
- real_bank: float32 [16384, 1024], P(('blk', 'rep')), may hold values from -6 to 6
- subset_rows: int32 [8192], P(('blk', 'rep')), may hold values from 0 to 511
Outputs:
- gradient: float32 [2048, 1024], P(('blk', 'rep'))
The draws below stay inside these ranges and needn't reach their ends.
All inputs are finite; a program needn't handle non-finite values.
Results may differ from the reference program's by a relative error of at most 0.0003.
Values sent between devices are 32-bit elements; how exact they have to be, the bound alone decides.
A program may use at most 128 MiB of HBM per device.

```python
import math
import jax
import jax.numpy as jnp
from jax import lax

D = 1024
REAL_DEV = 256
BANK_DEV = 512
M = 2048
R = 8192
BANK = 16384


class_count = 64


latent_count = 8


def class_centres(key, latent_scale, private_scale):
    direction_key = jax.random.fold_in(key, 101)
    position_key = jax.random.fold_in(key, 102)
    private_key = jax.random.fold_in(key, 103)
    directions = jnp.clip(jax.random.normal(direction_key, (latent_count, D), jnp.float32), -4.0, 4.0)
    positions = jnp.clip(jax.random.normal(position_key, (class_count, latent_count), jnp.float32), -4.0, 4.0)
    centres = private_scale * jnp.clip(jax.random.normal(private_key, (class_count, D), jnp.float32), -4.0, 4.0)
    for column in range(latent_count):
        centres = centres + latent_scale * positions[:, column:column + 1] * directions[column:column + 1, :]
    return centres


def draw_generated(key, part):
    centres = class_centres(key, 0.32, 0.7)
    key = jax.random.fold_in(key, 7)
    label_key = jax.random.fold_in(key, 1)
    noise_key = jax.random.fold_in(key, 2)
    labels = jax.random.randint(label_key, (M,), 0, class_count)
    picked = jnp.take(centres, labels, axis=0)
    noise = jnp.clip(jax.random.normal(noise_key, (M, D), jnp.float32), -4.0, 4.0)
    rows = 0.9 * picked + 0.55 * noise
    return jnp.clip(rows, -6.0, 6.0)


def draw_real_bank(key, part):
    centres = class_centres(key, 0.32, 0.7)
    key = jax.random.fold_in(key, 9)
    label_key = jax.random.fold_in(key, 1)
    noise_key = jax.random.fold_in(key, 2)
    labels = jax.random.randint(label_key, (BANK,), 0, class_count)
    picked = jnp.take(centres, labels, axis=0)
    noise = jnp.clip(jax.random.normal(noise_key, (BANK, D), jnp.float32), -4.0, 4.0)
    rows = picked + 0.7 * noise
    return jnp.clip(rows, -6.0, 6.0)


def place_ends(array, own_key, low, high):
    shape = array.shape
    spot = [jax.random.randint(jax.random.fold_in(own_key, axis), (), 0, shape[axis]) for axis in range(len(shape))]
    array = array.at[tuple(spot)].set(low)
    longest = shape.index(max(shape))
    spot[longest] = (spot[longest] + 1) % shape[longest]
    return array.at[tuple(spot)].set(high)


def setup_inputs(seed: int = 0) -> dict:
    streams_of = jax.random.split(jax.random.key(seed), 4)
    return {
        "generated": draw_generated(jax.random.fold_in(streams_of[3], 71), 0),
        "real_bank": draw_real_bank(jax.random.fold_in(streams_of[3], 71), 0),
        "subset_rows": place_ends(jax.random.randint(streams_of[2], (R,), 0, BANK_DEV), jax.random.fold_in(streams_of[2], 1), 0, BANK_DEV - 1).astype(jnp.int32),
    }


BANDS = (0.5, 1.0, 2.0)


def kernel_weight(dist, width):
    total = jnp.zeros_like(dist)
    for factor in BANDS:
        total = total + jnp.exp(-dist / (2.0 * factor * width)) / factor
    return total


def pair_parts(rows, others):
    row_norms = jnp.sum(rows * rows, axis=1)
    other_norms = jnp.sum(others * others, axis=1)
    inner = jnp.dot(rows, others.T, precision=lax.Precision.HIGHEST, preferred_element_type=jnp.float32)
    dist = jnp.maximum(row_norms[:, None] + other_norms[None, :] - 2.0 * inner, 0.0)
    weights = kernel_weight(dist, float(rows.shape[1]))
    weighted = jnp.dot(weights, others, precision=lax.Precision.HIGHEST, preferred_element_type=jnp.float32)
    return jnp.sum(weights, axis=1)[:, None] * rows - weighted


def reference(generated, real_bank, subset_rows):
    owner = jnp.arange(R, dtype=jnp.int32) // REAL_DEV
    real = real_bank[owner * BANK_DEV + subset_rows]
    step_rows = math.gcd(M, 512)
    blocks = generated.reshape(M // step_rows, step_rows, D)

    def one_block(rows):
        return pair_parts(rows, generated) / M - pair_parts(rows, real) / R

    return lax.map(one_block, blocks).reshape(M, D)
```

```python
import functools

import jax
import jax.numpy as jnp
from jax import lax
from jax.experimental import pallas as pl
from jax.experimental.pallas import tpu as pltpu
from jax.sharding import PartitionSpec as P

MESH = pl.DeviceIdType.MESH
GROUP = 4
PIECES = 4


def split(value):
    high = value.astype(jnp.bfloat16)
    return high, (value - high.astype(jnp.float32)).astype(jnp.bfloat16)


def dot(a, b, contract):
    return lax.dot_general(a, b, (contract, ((), ())), preferred_element_type=jnp.float32)


def product(a_high, a_low, b_high, b_low, contract):
    return (
        dot(a_high, b_high, contract)
        + dot(a_high, b_low, contract)
        + dot(a_low, b_high, contract)
    )


def kernel(
    sizes,
    rows_ref, gen_ref, bank_ref, out_ref,
    oth, oth_high, oth_low, oth_norm,
    gen, gen_high, gen_low, gen_norm, acc, total, from_hi, from_z,
    sib_send, sib_recv, far_send, far_recv, fwd_send, fwd_recv,
    z_send, z_recv, hi_send, hi_recv, red_hi_send, red_hi_recv, red_z_send, red_z_recv,
):
    blks, reps = sizes
    his = blks // GROUP
    n_gen, width = gen_ref.shape
    n_real = rows_ref.shape[0]
    piece = n_real // PIECES
    total_gen = n_gen * blks * reps
    total_real = n_real * blks * reps
    group = reps * n_gen

    blk, rep = lax.axis_index("blk"), lax.axis_index("rep")
    hi, lo = blk // GROUP, lax.rem(blk, GROUP)
    core, side = lax.rem(lo, 2), lo // 2
    sibling = (hi * GROUP + side * 2 + (1 - core), rep)
    across = (hi * GROUP + (1 - side) * 2 + core, rep)

    def z_partner(dz):
        return (blk, lax.rem(rep + dz, reps))

    def hi_partner(dh):
        return (lax.rem(hi + dh, his) * GROUP + lo, rep)

    half = n_real // 2
    starts = (0, n_real, 2 * n_real, 2 * n_real + GROUP * n_gen)
    c_gen, c_far = starts[2], starts[3]
    n_chunks = 5

    def far_rows(m, forwarded):
        chunk, part = divmod(m, PIECES // 2)
        return pl.ds(c_far + chunk * n_real + (half if forwarded else 0) + part * piece, piece)

    def gen_rows(slot):
        return pl.ds(c_gen + slot * n_gen, n_gen)

    def block(dh, dz):
        return pl.ds(dh * group + dz * n_gen, n_gen)

    def remote(src, dst, send, recv, device):
        return pltpu.make_async_remote_copy(
            src_ref=src, dst_ref=dst, send_sem=send, recv_sem=recv, device_id=device, device_id_type=MESH
        )

    partners = [sibling, across]
    partners += [z_partner(dz) for dz in range(1, reps)]
    partners += [hi_partner(dh) for dh in range(1, his)]
    barrier = pltpu.get_barrier_semaphore()
    for device in partners:
        pl.semaphore_signal(barrier, inc=1, device_id=device, device_id_type=MESH)

    def gather(i, carry):
        for k in range(8):
            p = i * 8 + k
            oth[pl.ds(p, 1), :] = bank_ref[pl.ds(rows_ref[p], 1), :]
        return carry

    lax.fori_loop(0, piece // 8, gather, 0)
    pl.semaphore_wait(barrier, len(partners))

    sent = []

    def start(copy):
        copy.start()
        sent.append(copy)
        return copy

    far_gen = start(remote(gen_ref, oth.at[gen_rows(2)], far_send.at[0], far_recv.at[0], across))
    z_copies, hi_copies = {}, {}
    z_order = [dz for dz in (2, 1, 3) if dz < reps] + list(range(4, reps))
    for dz in z_order:
        back = reps - dz
        z_copies[back] = start(
            remote(gen_ref, gen.at[block(0, back)], z_send.at[dz], z_recv.at[back], z_partner(dz))
        )
    for dh in range(1, his):
        back = his - dh
        hi_copies[back, 0] = start(
            remote(
                gen_ref, gen.at[block(back, 0)], hi_send.at[dh, 0], hi_recv.at[back, 0], hi_partner(dh)
            )
        )
    sib_gen = start(remote(gen_ref, oth.at[gen_rows(1)], sib_send.at[0], sib_recv.at[0], sibling))

    far_real = []
    for m in range(PIECES):
        if m > 0:
            lax.fori_loop(m * piece // 8, (m + 1) * piece // 8, gather, 0)
        far_real.append(
            start(
                remote(
                    oth.at[pl.ds(m * piece, piece)], oth.at[far_rows(m, False)],
                    far_send.at[1 + m], far_recv.at[1 + m], across,
                )
            )
        )
    sib_real = start(
        remote(oth.at[pl.ds(0, n_real)], oth.at[pl.ds(n_real, n_real)], sib_send.at[1], sib_recv.at[1], sibling)
    )

    def forward(rows, to, index):
        return start(remote(oth.at[rows], oth.at[to], fwd_send.at[index], fwd_recv.at[index], sibling))

    def prepare_other(start_row, count, chunk):
        rows = pl.ds(start_row, count)
        value = oth[rows, :]
        high, low = split(value)
        oth_high[rows, :] = high
        oth_low[rows, :] = low
        ones = jnp.ones((8, width), jnp.float32)
        oth_norm[chunk] = lax.dot_general(
            ones, value * value, (((1,), (1,)), ((), ())),
            precision=lax.Precision.HIGHEST, preferred_element_type=jnp.float32,
        )

    def prepare_gen(rows):
        value = gen[rows, :]
        high, low = split(value)
        gen_high[rows, :] = high
        gen_low[rows, :] = low
        gen_norm[rows, :] = jnp.sum(value * value, axis=1, keepdims=True)

    def add_pairs(row_start, other_start, chunk, scale, first=False):
        rows = pl.ds(row_start, group)
        others = pl.ds(other_start, n_real)
        inner = product(
            gen_high[rows, :], gen_low[rows, :], oth_high[others, :], oth_low[others, :], ((1,), (1,))
        )
        dist = jnp.maximum(gen_norm[rows, :] + oth_norm[chunk, 0:1, :] - 2.0 * inner, 0.0)
        wide = jnp.exp(dist * (-1.0 / (4.0 * width)))
        middle = wide * wide
        weight = (2.0 * (middle * middle) + middle + 0.5 * wide) * scale
        sums = jnp.sum(weight, axis=1, keepdims=True)
        w_high, w_low = split(weight)
        step = 256
        for column in range(0, width, step):
            columns = pl.ds(column, step)
            part = product(w_high, w_low, oth_high[others, columns], oth_low[others, columns], ((1,), (0,)))
            acc[rows, columns] = part if first else acc[rows, columns] + part
        total[rows, :] = sums if first else total[rows, :] + sums

    def finish(row_start):
        rows = pl.ds(row_start, group)
        acc[rows, :] = total[rows, :] * gen[rows, :] - acc[rows, :]

    self_scale, cross_scale = 1.0 / total_gen, -1.0 / total_real

    gen[block(0, 0), :] = gen_ref[...]
    prepare_gen(block(0, 0))
    oth[gen_rows(0), :] = gen_ref[...]
    prepare_other(0, n_real, 0)

    for dz in z_order:
        z_copies[dz].wait_recv()
        for dh in range(1, his):
            back = his - dh
            hi_copies[back, dz] = start(
                remote(
                    gen.at[block(0, dz)], gen.at[block(back, dz)],
                    hi_send.at[dh, dz], hi_recv.at[back, dz], hi_partner(dh),
                )
            )
        prepare_gen(block(0, dz))
    far_gen.wait_recv()
    forwards = [forward(gen_rows(2), gen_rows(3), 0)]

    add_pairs(0, 0, 0, cross_scale, first=True)
    sib_gen.wait_recv()
    sib_real.wait_recv()
    prepare_other(n_real, n_real, 1)
    add_pairs(0, n_real, 1, cross_scale)
    forwards[0].wait_recv()
    prepare_other(c_gen, GROUP * n_gen, 2)
    add_pairs(0, c_gen, 2, self_scale)

    def take_far(m):
        far_real[m].wait_recv()
        forwards.append(forward(far_rows(m, False), far_rows(m, True), 1 + m))

    for m in range(PIECES // 2):
        take_far(m)

    for dh in range(1, his):
        for dz in range(reps):
            hi_copies[dh, dz].wait_recv()

    def later_rows(dh, carry):
        row_start = pl.multiple_of(dh * group, group)
        for dz in range(reps):
            prepare_gen(pl.ds(row_start + dz * n_gen, n_gen))
        add_pairs(row_start, 0, 0, cross_scale, first=True)

        def chunk_pairs(c, inner_carry):
            scale = jnp.where(c == 2, self_scale, cross_scale)
            add_pairs(row_start, pl.multiple_of(c * n_real, n_real), c, scale)
            return inner_carry

        lax.fori_loop(1, 3, chunk_pairs, 0)
        return carry

    lax.fori_loop(1, his, later_rows, 0)

    for m in range(PIECES // 2):
        forwards[1 + m].wait_recv()
    prepare_other(c_far, n_real, 3)

    def third_chunk(dh, carry):
        add_pairs(pl.multiple_of(dh * group, group), c_far, 3, cross_scale)
        return carry

    lax.fori_loop(0, his, third_chunk, 0)

    for m in range(PIECES // 2, PIECES):
        take_far(m)
    for m in range(PIECES // 2, PIECES):
        forwards[1 + m].wait_recv()
    prepare_other(c_far + n_real, n_real, 4)

    red_hi = {}
    for dh in range(1, his):
        back = his - dh
        add_pairs(dh * group, c_far + n_real, 4, cross_scale)
        finish(dh * group)
        for dz in z_order + [0]:
            red_hi[back, dz] = start(
                remote(
                    acc.at[block(dh, dz)], from_hi.at[back, dz],
                    red_hi_send.at[dh, dz], red_hi_recv.at[back, dz], hi_partner(dh),
                )
            )
    add_pairs(0, c_far + n_real, 4, cross_scale)
    finish(0)

    red_z = {}
    for dz in z_order + [0]:
        for dh in range(1, his):
            red_hi[dh, dz].wait_recv()
            acc[block(0, dz), :] = acc[block(0, dz), :] + from_hi[dh, dz]
        if dz > 0:
            back = reps - dz
            red_z[back] = start(
                remote(
                    acc.at[block(0, dz)], from_z.at[back],
                    red_z_send.at[dz], red_z_recv.at[back], z_partner(dz),
                )
            )
    result = acc[block(0, 0), :]
    for dz in z_order:
        red_z[dz].wait_recv()
        result = result + from_z[dz]
    out_ref[...] = result

    for copy in sent:
        copy.wait_send()


def solution(mesh):
    blks, reps = mesh.shape["blk"], mesh.shape["rep"]
    his = blks // GROUP

    def on_device(generated, real_bank, subset_rows):
        n_gen, width = generated.shape
        n_real = subset_rows.shape[0]
        n_other = 5 * n_real
        n_rows = his * reps * n_gen
        dma = pltpu.SemaphoreType.DMA
        vmem = pl.BlockSpec(memory_space=pltpu.VMEM)
        pairs = n_rows * n_other
        return pl.pallas_call(
            functools.partial(kernel, (blks, reps)),
            out_shape=jax.ShapeDtypeStruct((n_gen, width), jnp.float32),
            in_specs=[pl.BlockSpec(memory_space=pltpu.SMEM), vmem, vmem],
            out_specs=vmem,
            scratch_shapes=[
                pltpu.VMEM((n_other, width), jnp.float32),
                pltpu.VMEM((n_other, width), jnp.bfloat16),
                pltpu.VMEM((n_other, width), jnp.bfloat16),
                pltpu.VMEM((5, 8, n_real), jnp.float32),
                pltpu.VMEM((n_rows, width), jnp.float32),
                pltpu.VMEM((n_rows, width), jnp.bfloat16),
                pltpu.VMEM((n_rows, width), jnp.bfloat16),
                pltpu.VMEM((n_rows, 1), jnp.float32),
                pltpu.VMEM((n_rows, width), jnp.float32),
                pltpu.VMEM((n_rows, 1), jnp.float32),
                pltpu.VMEM((his, reps, n_gen, width), jnp.float32),
                pltpu.VMEM((reps, n_gen, width), jnp.float32),
                dma((2,)), dma((2,)),
                dma((1 + PIECES,)), dma((1 + PIECES,)),
                dma((1 + PIECES,)), dma((1 + PIECES,)),
                dma((reps,)), dma((reps,)),
                dma((his, reps)), dma((his, reps)),
                dma((his, reps)), dma((his, reps)),
                dma((reps,)), dma((reps,)),
            ],
            compiler_params=pltpu.CompilerParams(
                collective_id=0, has_side_effects=True, vmem_limit_bytes=60 * 1024 * 1024
            ),
            cost_estimate=pl.CostEstimate(
                flops=12 * pairs * width, bytes_accessed=4 * 1024 * width, transcendentals=pairs
            ),
        )(subset_rows, generated, real_bank)

    in_specs = (P(("blk", "rep"), None), P(("blk", "rep"), None), P(("blk", "rep")))
    return jax.shard_map(
        on_device, mesh=mesh, in_specs=in_specs, out_specs=P(("blk", "rep"), None), check_vma=False
    )
```

```python
import functools

import jax
import jax.numpy as jnp
from jax import lax
from jax.experimental import pallas as pl
from jax.experimental.pallas import tpu as pltpu
from jax.sharding import PartitionSpec as P

MESH = pl.DeviceIdType.MESH
GROUP = 4
PAIR = 2
PIECES = 4


def split(value):
    high = value.astype(jnp.bfloat16)
    return high, (value - high.astype(jnp.float32)).astype(jnp.bfloat16)


def dot(a, b, contract):
    return lax.dot_general(a, b, (contract, ((), ())), preferred_element_type=jnp.float32)


def product(a_high, a_low, b_high, b_low, contract):
    return (
        dot(a_high, b_high, contract)
        + dot(a_high, b_low, contract)
        + dot(a_low, b_high, contract)
    )


def kernel(
    sizes,
    rows_ref, gen_ref, bank_ref, out_ref, bank, bank_sem,
    oth, oth_high, oth_low, oth_norm,
    gen, gen_high, gen_low, gen_norm, acc, total, from_hi, from_z,
    sib_send, sib_recv, far_send, far_recv, fwd_send, fwd_recv,
    z_send, z_recv, hi_send, hi_recv, red_hi_send, red_hi_recv, red_z_send, red_z_recv,
):
    blks, reps = sizes
    his = blks // GROUP
    n_gen, width = gen_ref.shape
    n_real = rows_ref.shape[0]
    piece = n_real // PIECES
    total_gen = n_gen * blks * reps
    total_real = n_real * blks * reps
    tile = PAIR * n_gen
    near_tiles = reps // PAIR
    n_tiles = his * near_tiles

    blk, rep = lax.axis_index("blk"), lax.axis_index("rep")
    hi, lo = blk // GROUP, lax.rem(blk, GROUP)
    core, side = lax.rem(lo, 2), lo // 2
    sibling = (hi * GROUP + side * 2 + (1 - core), rep)
    across = (hi * GROUP + (1 - side) * 2 + core, rep)

    def z_partner(dz):
        return (blk, lax.rem(rep + dz, reps))

    def hi_partner(dh):
        return (lax.rem(hi + dh, his) * GROUP + lo, rep)

    half = n_real // 2
    c_gen, c_far = 2 * n_real, 3 * n_real

    def far_rows(m, forwarded):
        chunk, part = divmod(m, PIECES // 2)
        return pl.ds(c_far + chunk * n_real + (half if forwarded else 0) + part * piece, piece)

    def gen_rows(slot):
        return pl.ds(c_gen + slot * n_gen, n_gen)

    def block(dh, dz):
        return pl.ds(pl.multiple_of((dh * reps + dz) * n_gen, n_gen), n_gen)

    def remote(src, dst, send, recv, device):
        return pltpu.make_async_remote_copy(
            src_ref=src, dst_ref=dst, send_sem=send, recv_sem=recv, device_id=device, device_id_type=MESH
        )

    def z_copy(dz):
        back = reps - dz
        return remote(gen_ref, gen.at[block(0, back)], z_send.at[dz], z_recv.at[back], z_partner(dz))

    def hi_copy(dh, dz, src):
        back = his - dh
        return remote(src, gen.at[block(back, dz)], hi_send.at[dh, dz], hi_recv.at[back, dz], hi_partner(dh))

    def far_gen():
        return remote(gen_ref, oth.at[gen_rows(2)], far_send.at[0], far_recv.at[0], across)

    def far_real(m):
        return remote(
            oth.at[pl.ds(m * piece, piece)], oth.at[far_rows(m, False)],
            far_send.at[1 + m], far_recv.at[1 + m], across,
        )

    def sib_gen():
        return remote(gen_ref, oth.at[gen_rows(1)], sib_send.at[0], sib_recv.at[0], sibling)

    def sib_real():
        return remote(
            oth.at[pl.ds(0, n_real)], oth.at[pl.ds(n_real, n_real)], sib_send.at[1], sib_recv.at[1], sibling
        )

    def forward_gen():
        return remote(oth.at[gen_rows(2)], oth.at[gen_rows(3)], fwd_send.at[0], fwd_recv.at[0], sibling)

    def forward_real(m):
        return remote(
            oth.at[far_rows(m, False)], oth.at[far_rows(m, True)],
            fwd_send.at[1 + m], fwd_recv.at[1 + m], sibling,
        )

    def red_hi(dh, dz):
        back = his - dh
        return remote(
            acc.at[block(dh, dz)], from_hi.at[back, dz],
            red_hi_send.at[dh, dz], red_hi_recv.at[back, dz], hi_partner(dh),
        )

    def red_z(dz):
        back = reps - dz
        return remote(
            acc.at[block(0, dz)], from_z.at[back], red_z_send.at[dz], red_z_recv.at[back], z_partner(dz)
        )

    load_bank = pltpu.make_async_copy(bank_ref, bank, bank_sem)
    load_bank.start()
    partners = [sibling, across]
    partners += [z_partner(dz) for dz in range(1, reps)]
    partners += [hi_partner(dh) for dh in range(1, his)]
    barrier = pltpu.get_barrier_semaphore()
    for device in partners:
        pl.semaphore_signal(barrier, inc=1, device_id=device, device_id_type=MESH)
    load_bank.wait()

    def gather(i, carry):
        for k in range(8):
            p = i * 8 + k
            oth[pl.ds(p, 1), :] = bank[pl.ds(rows_ref[p], 1), :]
        return carry

    lax.fori_loop(0, piece // 8, gather, 0)
    pl.semaphore_wait(barrier, len(partners))

    far_gen().start()
    z_copy(1).start()
    for dh in range(1, his):
        hi_copy(dh, 0, gen_ref).start()
    for dz in range(2, reps):
        z_copy(dz).start()
    sib_gen().start()

    far_real(0).start()
    for m in range(1, PIECES):
        lax.fori_loop(m * piece // 8, (m + 1) * piece // 8, gather, 0)
        far_real(m).start()
    sib_real().start()

    def prepare_other(chunk):
        rows = pl.ds(chunk * n_real, n_real)
        value = oth[rows, :]
        high, low = split(value)
        oth_high[rows, :] = high
        oth_low[rows, :] = low
        norm = jnp.sum(value * value, axis=1, keepdims=True)
        oth_norm[chunk] = jnp.broadcast_to(norm, (n_real, 128)).T[0:8, :]

    def prepare_gen(rows):
        value = gen[rows, :]
        high, low = split(value)
        gen_high[rows, :] = high
        gen_low[rows, :] = low
        gen_norm[rows, :] = jnp.sum(value * value, axis=1, keepdims=True)

    def tile_rows(q):
        return pl.ds(pl.multiple_of(q * tile, tile), tile)

    def add_pairs(q, chunk, scale):
        rows = tile_rows(q)
        others = pl.ds(pl.multiple_of(chunk * n_real, n_real), n_real)
        inner = product(
            gen_high[rows, :], gen_low[rows, :], oth_high[others, :], oth_low[others, :], ((1,), (1,))
        )
        dist = jnp.maximum(gen_norm[rows, :] + oth_norm[chunk, 0:1, :] - 2.0 * inner, 0.0)
        wide = jnp.exp(dist * (-1.0 / (4.0 * width)))
        middle = wide * wide
        weight = (2.0 * (middle * middle) + middle + 0.5 * wide) * scale
        total[rows, :] += jnp.sum(weight, axis=1, keepdims=True)
        w_high, w_low = split(weight)
        step = 256
        for column in range(0, width, step):
            columns = pl.ds(column, step)
            acc[rows, columns] += product(
                w_high, w_low, oth_high[others, columns], oth_low[others, columns], ((1,), (0,))
            )

    self_scale, cross_scale = 1.0 / total_gen, -1.0 / total_real

    def take_far(m):
        far_real(m).wait_recv()
        forward_real(m).start()

    def take_z(dz):
        z_copy(reps - dz).wait_recv()
        for dh in range(1, his):
            hi_copy(dh, dz, gen.at[block(0, dz)]).start()

    gen[block(0, 0), :] = gen_ref[...]
    oth[gen_rows(0), :] = gen_ref[...]
    prepare_other(0)
    far_gen().wait_recv()
    forward_gen().start()
    for dz in range(1, PAIR):
        take_z(dz)
    sib_gen().wait_recv()
    sib_real().wait_recv()
    prepare_other(1)
    forward_gen().wait_recv()
    prepare_other(2)

    def first_chunks(q, carry):
        for k in range(1, near_tiles):

            @pl.when(q == k)
            def _():
                for dz in range(k * PAIR, (k + 1) * PAIR):
                    take_z(dz)

        @pl.when(q == 1)
        def _():
            for m in range(PIECES // 2):
                take_far(m)

        @pl.when(q >= near_tiles)
        def _():
            for i in range(PAIR):
                dh, dz = q // near_tiles, lax.rem(q, near_tiles) * PAIR + i
                hi_copy(his - dh, dz, gen_ref).wait_recv()

        rows = tile_rows(q)
        prepare_gen(rows)
        acc[rows, :] = jnp.zeros((tile, width), jnp.float32)
        total[rows, :] = jnp.zeros((tile, 1), jnp.float32)

        def chunk_pairs(chunk, inner_carry):
            add_pairs(q, chunk, jnp.where(chunk == 2, self_scale, cross_scale))
            return inner_carry

        lax.fori_loop(0, 3, chunk_pairs, 0)
        return carry

    lax.fori_loop(0, n_tiles, first_chunks, 0)

    take_far(PIECES // 2)
    for m in range(PIECES // 2):
        forward_real(m).wait_recv()
    prepare_other(3)

    def third_chunk(q, carry):
        add_pairs(q, 3, cross_scale)
        return carry

    lax.fori_loop(0, n_tiles, third_chunk, 0)

    for m in range(PIECES // 2 + 1, PIECES):
        take_far(m)
    for m in range(PIECES // 2, PIECES):
        forward_real(m).wait_recv()
    prepare_other(4)

    def last_chunk(i, carry):
        q = n_tiles - 1 - i
        add_pairs(q, 4, cross_scale)
        rows = tile_rows(q)
        acc[rows, :] = total[rows, :] * gen[rows, :] - acc[rows, :]

        @pl.when(q >= near_tiles)
        def _():
            for k in reversed(range(PAIR)):
                dh, dz = q // near_tiles, lax.rem(q, near_tiles) * PAIR + k
                red_hi(dh, dz).start()

        return carry

    lax.fori_loop(0, n_tiles, last_chunk, 0)

    for dz in reversed(range(reps)):
        for dh in range(1, his):
            red_hi(his - dh, dz).wait_recv()
            acc[block(0, dz), :] += from_hi[dh, dz]
        if dz > 0:
            red_z(dz).start()
    result = acc[block(0, 0), :]
    for dz in reversed(range(1, reps)):
        red_z(reps - dz).wait_recv()
        result = result + from_z[dz]
    out_ref[...] = result

    sent = [far_gen(), sib_gen(), sib_real(), forward_gen()]
    sent += [far_real(m) for m in range(PIECES)] + [forward_real(m) for m in range(PIECES)]
    sent += [z_copy(dz) for dz in range(1, reps)] + [red_z(dz) for dz in range(1, reps)]
    sent += [hi_copy(dh, dz, gen_ref) for dh in range(1, his) for dz in range(reps)]
    sent += [red_hi(dh, dz) for dh in range(1, his) for dz in range(reps)]
    for copy in sent:
        copy.wait_send()


def solution(mesh):
    blks, reps = mesh.shape["blk"], mesh.shape["rep"]
    his = blks // GROUP

    def on_device(generated, real_bank, subset_rows):
        n_gen, width = generated.shape
        n_real = subset_rows.shape[0]
        n_other = 5 * n_real
        n_rows = his * reps * n_gen
        dma = pltpu.SemaphoreType.DMA
        vmem = pl.BlockSpec(memory_space=pltpu.VMEM)
        pairs = n_rows * n_other
        return pl.pallas_call(
            functools.partial(kernel, (blks, reps)),
            out_shape=jax.ShapeDtypeStruct((n_gen, width), jnp.float32),
            in_specs=[pl.BlockSpec(memory_space=pltpu.SMEM), vmem, pl.BlockSpec(memory_space=pl.ANY)],
            out_specs=vmem,
            scratch_shapes=[
                pltpu.VMEM(real_bank.shape, jnp.float32),
                dma(()),
                pltpu.VMEM((n_other, width), jnp.float32),
                pltpu.VMEM((n_other, width), jnp.bfloat16),
                pltpu.VMEM((n_other, width), jnp.bfloat16),
                pltpu.VMEM((5, 8, n_real), jnp.float32),
                pltpu.VMEM((n_rows, width), jnp.float32),
                pltpu.VMEM((n_rows, width), jnp.bfloat16),
                pltpu.VMEM((n_rows, width), jnp.bfloat16),
                pltpu.VMEM((n_rows, 1), jnp.float32),
                pltpu.VMEM((n_rows, width), jnp.float32),
                pltpu.VMEM((n_rows, 1), jnp.float32),
                pltpu.VMEM((his, reps, n_gen, width), jnp.float32),
                pltpu.VMEM((reps, n_gen, width), jnp.float32),
                dma((2,)), dma((2,)),
                dma((1 + PIECES,)), dma((1 + PIECES,)),
                dma((1 + PIECES,)), dma((1 + PIECES,)),
                dma((reps,)), dma((reps,)),
                dma((his, reps)), dma((his, reps)),
                dma((his, reps)), dma((his, reps)),
                dma((reps,)), dma((reps,)),
            ],
            compiler_params=pltpu.CompilerParams(
                collective_id=0, has_side_effects=True, vmem_limit_bytes=60 * 1024 * 1024
            ),
            cost_estimate=pl.CostEstimate(
                flops=12 * pairs * width, bytes_accessed=4 * 1024 * width, transcendentals=pairs
            ),
        )(subset_rows, generated, real_bank)

    in_specs = (P(("blk", "rep"), None), P(("blk", "rep"), None), P(("blk", "rep")))
    return jax.shard_map(
        on_device, mesh=mesh, in_specs=in_specs, out_specs=P(("blk", "rep"), None), check_vma=False
    )
```

```python
import functools

import jax
import jax.numpy as jnp
from jax import lax
from jax.experimental import pallas as pl
from jax.experimental.pallas import tpu as pltpu
from jax.sharding import PartitionSpec as P

MESH = pl.DeviceIdType.MESH
GROUP = 4
PIECES = 4


def split(value):
    high = value.astype(jnp.bfloat16)
    return high, (value - high.astype(jnp.float32)).astype(jnp.bfloat16)


def dot(a, b, contract):
    return lax.dot_general(a, b, (contract, ((), ())), preferred_element_type=jnp.float32)


def product(a_both, a_high, b_high, b_low, contract):
    rows = a_high.shape[0]
    both = dot(a_both, b_high, contract)
    return both[:rows] + (both[rows:] + dot(a_high, b_low, contract))


def kernel(
    sizes,
    rows_ref, gen_ref, bank_ref, out_ref, bank, bank_sem,
    oth, oth_high, oth_low, oth_norm,
    gen, gen_both, gen_norm, acc, total, from_hi, from_z,
    sib_send, sib_recv, far_send, far_recv, fwd_send, fwd_recv,
    z_send, z_recv, hi_send, hi_recv, red_hi_send, red_hi_recv, red_z_send, red_z_recv,
):
    blks, reps = sizes
    his = blks // GROUP
    n_gen, width = gen_ref.shape
    n_real = rows_ref.shape[0]
    piece = n_real // PIECES
    total_gen = n_gen * blks * reps
    total_real = n_real * blks * reps
    tile = reps * n_gen

    blk, rep = lax.axis_index("blk"), lax.axis_index("rep")
    hi, lo = blk // GROUP, lax.rem(blk, GROUP)
    core, side = lax.rem(lo, 2), lo // 2
    sibling = (hi * GROUP + side * 2 + (1 - core), rep)
    across = (hi * GROUP + (1 - side) * 2 + core, rep)

    def z_partner(dz):
        return (blk, lax.rem(rep + dz, reps))

    def hi_partner(dh):
        return (lax.rem(hi + dh, his) * GROUP + lo, rep)

    half = n_real // 2
    c_gen, c_far = 2 * n_real, 3 * n_real

    def far_rows(m, forwarded):
        chunk, part = divmod(m, PIECES // 2)
        return pl.ds(c_far + chunk * n_real + (half if forwarded else 0) + part * piece, piece)

    def gen_rows(slot):
        return pl.ds(c_gen + slot * n_gen, n_gen)

    def block(dh, dz):
        return pl.ds(pl.multiple_of((dh * reps + dz) * n_gen, n_gen), n_gen)

    def remote(src, dst, send, recv, device):
        return pltpu.make_async_remote_copy(
            src_ref=src, dst_ref=dst, send_sem=send, recv_sem=recv, device_id=device, device_id_type=MESH
        )

    def z_copy(dz):
        back = reps - dz
        return remote(gen_ref, gen.at[block(0, back)], z_send.at[dz], z_recv.at[back], z_partner(dz))

    def hi_copy(dh, dz, src):
        back = his - dh
        return remote(src, gen.at[block(back, dz)], hi_send.at[dh, dz], hi_recv.at[back, dz], hi_partner(dh))

    def far_gen():
        return remote(gen_ref, oth.at[gen_rows(2)], far_send.at[0], far_recv.at[0], across)

    def far_real(m):
        return remote(
            oth.at[pl.ds(m * piece, piece)], oth.at[far_rows(m, False)],
            far_send.at[1 + m], far_recv.at[1 + m], across,
        )

    def sib_gen():
        return remote(gen_ref, oth.at[gen_rows(1)], sib_send.at[0], sib_recv.at[0], sibling)

    def sib_real():
        return remote(
            oth.at[pl.ds(0, n_real)], oth.at[pl.ds(n_real, n_real)], sib_send.at[1], sib_recv.at[1], sibling
        )

    def forward_gen():
        return remote(oth.at[gen_rows(2)], oth.at[gen_rows(3)], fwd_send.at[0], fwd_recv.at[0], sibling)

    def forward_real(m):
        return remote(
            oth.at[far_rows(m, False)], oth.at[far_rows(m, True)],
            fwd_send.at[1 + m], fwd_recv.at[1 + m], sibling,
        )

    def red_hi(dh, dz):
        back = his - dh
        return remote(
            acc.at[block(dh, dz)], from_hi.at[back, dz],
            red_hi_send.at[dh, dz], red_hi_recv.at[back, dz], hi_partner(dh),
        )

    def red_z(dz):
        back = reps - dz
        return remote(
            acc.at[block(0, dz)], from_z.at[back], red_z_send.at[dz], red_z_recv.at[back], z_partner(dz)
        )

    load_bank = pltpu.make_async_copy(bank_ref, bank, bank_sem)
    load_bank.start()
    partners = [sibling, across]
    partners += [z_partner(dz) for dz in range(1, reps)]
    partners += [hi_partner(dh) for dh in range(1, his)]
    barrier = pltpu.get_barrier_semaphore()
    for device in partners:
        pl.semaphore_signal(barrier, inc=1, device_id=device, device_id_type=MESH)
    load_bank.wait()

    def gather(i, carry):
        picked = [bank[pl.ds(rows_ref[i * 8 + k], 1), :] for k in range(8)]
        for k in range(8):
            p = i * 8 + k
            oth[pl.ds(p, 1), :] = picked[k]
        return carry

    lax.fori_loop(0, piece // 8, gather, 0)
    pl.semaphore_wait(barrier, len(partners))

    far_gen().start()
    z_copy(1).start()
    for dh in range(1, his):
        hi_copy(dh, 0, gen_ref).start()
    for dz in range(2, reps):
        z_copy(dz).start()
    sib_gen().start()

    far_real(0).start()
    for m in range(1, PIECES):
        lax.fori_loop(m * piece // 8, (m + 1) * piece // 8, gather, 0)
        far_real(m).start()
    sib_real().start()

    def prepare_other(chunk):
        rows = pl.ds(chunk * n_real, n_real)
        value = oth[rows, :]
        high, low = split(value)
        oth_high[rows, :] = high
        oth_low[rows, :] = low
        norm = jnp.sum(value * value, axis=1, keepdims=True)
        oth_norm[chunk] = jnp.broadcast_to(norm, (n_real, 128)).T[0:8, :]

    def prepare_gen(q):
        rows = tile_rows(q)
        value = gen[rows, :]
        high, low = split(value)
        start = pl.multiple_of(2 * tile * q, tile)
        gen_both[pl.ds(start, tile), :] = high
        gen_both[pl.ds(pl.multiple_of(start + tile, tile), tile), :] = low
        gen_norm[rows, :] = jnp.sum(value * value, axis=1, keepdims=True)

    def tile_rows(q):
        return pl.ds(pl.multiple_of(q * tile, tile), tile)

    def add_pairs(q, chunk, scale):
        rows = tile_rows(q)
        others = pl.ds(pl.multiple_of(chunk * n_real, n_real), n_real)
        start = pl.multiple_of(2 * tile * q, tile)
        inner = product(
            gen_both[pl.ds(start, 2 * tile), :], gen_both[pl.ds(start, tile), :],
            oth_high[others, :], oth_low[others, :], ((1,), (1,)),
        )
        dist = jnp.maximum(gen_norm[rows, :] + oth_norm[chunk, 0:1, :] - 2.0 * inner, 0.0)
        wide = jnp.exp(dist * (-1.0 / (4.0 * width)))
        middle = wide * wide
        weight = (2.0 * (middle * middle) + middle + 0.5 * wide) * scale
        total[rows, :] += jnp.sum(weight, axis=1, keepdims=True)
        w_high, w_low = split(weight)
        w_both = jnp.concatenate([w_high, w_low], axis=0)
        step = 256
        for column in range(0, width, step):
            columns = pl.ds(column, step)
            acc[rows, columns] += product(
                w_both, w_high, oth_high[others, columns], oth_low[others, columns], ((1,), (0,))
            )

    self_scale, cross_scale = 1.0 / total_gen, -1.0 / total_real

    def take_far(m):
        far_real(m).wait_recv()
        forward_real(m).start()

    def take_z(dz):
        z_copy(reps - dz).wait_recv()
        for dh in range(1, his):
            hi_copy(dh, dz, gen.at[block(0, dz)]).start()

    gen[block(0, 0), :] = gen_ref[...]
    oth[gen_rows(0), :] = gen_ref[...]
    prepare_other(0)
    far_gen().wait_recv()
    forward_gen().start()
    for dz in range(1, reps):
        take_z(dz)
    sib_gen().wait_recv()
    sib_real().wait_recv()
    prepare_other(1)
    forward_gen().wait_recv()
    prepare_other(2)

    def first_chunks(q, carry):
        @pl.when(q == 1)
        def _():
            for m in range(PIECES // 2):
                take_far(m)

        @pl.when(q >= 1)
        def _():
            for dz in range(reps):
                hi_copy(his - q, dz, gen_ref).wait_recv()

        rows = tile_rows(q)
        prepare_gen(q)
        acc[rows, :] = jnp.zeros((tile, width), jnp.float32)
        total[rows, :] = jnp.zeros((tile, 1), jnp.float32)

        def chunk_pairs(chunk, inner_carry):
            add_pairs(q, chunk, jnp.where(chunk == 2, self_scale, cross_scale))
            return inner_carry

        lax.fori_loop(0, 3, chunk_pairs, 0)
        return carry

    lax.fori_loop(0, his, first_chunks, 0)

    take_far(PIECES // 2)
    for m in range(PIECES // 2):
        forward_real(m).wait_recv()
    prepare_other(3)

    def third_chunk(q, carry):
        add_pairs(q, 3, cross_scale)
        return carry

    lax.fori_loop(0, his, third_chunk, 0)

    for m in range(PIECES // 2 + 1, PIECES):
        take_far(m)
    for m in range(PIECES // 2, PIECES):
        forward_real(m).wait_recv()
    prepare_other(4)

    def last_chunk(i, carry):
        q = his - 1 - i
        add_pairs(q, 4, cross_scale)
        rows = tile_rows(q)
        acc[rows, :] = total[rows, :] * gen[rows, :] - acc[rows, :]

        @pl.when(q >= 1)
        def _():
            for dz in reversed(range(reps)):
                red_hi(q, dz).start()

        return carry

    lax.fori_loop(0, his, last_chunk, 0)

    for dz in reversed(range(reps)):
        for dh in range(1, his):
            red_hi(his - dh, dz).wait_recv()
            acc[block(0, dz), :] += from_hi[dh, dz]
        if dz > 0:
            red_z(dz).start()
    result = acc[block(0, 0), :]
    for dz in reversed(range(1, reps)):
        red_z(reps - dz).wait_recv()
        result = result + from_z[dz]
    out_ref[...] = result

    sent = [far_gen(), sib_gen(), sib_real(), forward_gen()]
    sent += [far_real(m) for m in range(PIECES)] + [forward_real(m) for m in range(PIECES)]
    sent += [z_copy(dz) for dz in range(1, reps)] + [red_z(dz) for dz in range(1, reps)]
    sent += [hi_copy(dh, dz, gen_ref) for dh in range(1, his) for dz in range(reps)]
    sent += [red_hi(dh, dz) for dh in range(1, his) for dz in range(reps)]
    for copy in sent:
        copy.wait_send()


def solution(mesh):
    blks, reps = mesh.shape["blk"], mesh.shape["rep"]
    his = blks // GROUP

    def on_device(generated, real_bank, subset_rows):
        n_gen, width = generated.shape
        n_real = subset_rows.shape[0]
        n_other = 5 * n_real
        n_rows = his * reps * n_gen
        dma = pltpu.SemaphoreType.DMA
        vmem = pl.BlockSpec(memory_space=pltpu.VMEM)
        pairs = n_rows * n_other
        return pl.pallas_call(
            functools.partial(kernel, (blks, reps)),
            out_shape=jax.ShapeDtypeStruct((n_gen, width), jnp.float32),
            in_specs=[pl.BlockSpec(memory_space=pltpu.SMEM), vmem, pl.BlockSpec(memory_space=pl.ANY)],
            out_specs=vmem,
            scratch_shapes=[
                pltpu.VMEM(real_bank.shape, jnp.float32),
                dma(()),
                pltpu.VMEM((n_other, width), jnp.float32),
                pltpu.VMEM((n_other, width), jnp.bfloat16),
                pltpu.VMEM((n_other, width), jnp.bfloat16),
                pltpu.VMEM((5, 8, n_real), jnp.float32),
                pltpu.VMEM((n_rows, width), jnp.float32),
                pltpu.VMEM((2 * n_rows, width), jnp.bfloat16),
                pltpu.VMEM((n_rows, 1), jnp.float32),
                pltpu.VMEM((n_rows, width), jnp.float32),
                pltpu.VMEM((n_rows, 1), jnp.float32),
                pltpu.VMEM((his, reps, n_gen, width), jnp.float32),
                pltpu.VMEM((reps, n_gen, width), jnp.float32),
                dma((2,)), dma((2,)),
                dma((1 + PIECES,)), dma((1 + PIECES,)),
                dma((1 + PIECES,)), dma((1 + PIECES,)),
                dma((reps,)), dma((reps,)),
                dma((his, reps)), dma((his, reps)),
                dma((his, reps)), dma((his, reps)),
                dma((reps,)), dma((reps,)),
            ],
            compiler_params=pltpu.CompilerParams(
                collective_id=0, has_side_effects=True, vmem_limit_bytes=60 * 1024 * 1024
            ),
            cost_estimate=pl.CostEstimate(
                flops=12 * pairs * width, bytes_accessed=4 * 1024 * width, transcendentals=pairs
            ),
        )(subset_rows, generated, real_bank)

    in_specs = (P(("blk", "rep"), None), P(("blk", "rep"), None), P(("blk", "rep")))
    return jax.shard_map(
        on_device, mesh=mesh, in_specs=in_specs, out_specs=P(("blk", "rep"), None), check_vma=False
    )
```

```python
import functools

import jax
import jax.numpy as jnp
from jax import lax
from jax.experimental import pallas as pl
from jax.experimental.pallas import tpu as pltpu
from jax.sharding import PartitionSpec as P

MESH = pl.DeviceIdType.MESH
GROUP = 4
ORDER = (0, 1, 3, 2)
PIECES = 4


def split(value):
    high = value.astype(jnp.bfloat16)
    return high, (value - high.astype(jnp.float32)).astype(jnp.bfloat16)


def dot(a, b, contract):
    return lax.dot_general(a, b, (contract, ((), ())), preferred_element_type=jnp.float32)


def product(a_both, a_high, b_high, b_low, contract):
    rows = a_high.shape[0]
    both = dot(a_both, b_high, contract)
    return both[:rows] + (both[rows:] + dot(a_high, b_low, contract))


def kernel(
    sizes,
    rows_ref, gen_ref, bank_ref, out_ref, bank, bank_sem,
    oth, oth_high, oth_low, oth_norm,
    gen, gen_both, gen_norm, acc, total, from_hi, from_z,
    sib_send, sib_recv, far_send, far_recv, fwd_send, fwd_recv,
    z_send, z_recv, hi_send, hi_recv, red_hi_send, red_hi_recv, red_z_send, red_z_recv,
):
    blks, reps = sizes
    his = blks // GROUP
    n_gen, width = gen_ref.shape
    n_real = rows_ref.shape[0]
    piece = n_real // PIECES
    total_gen = n_gen * blks * reps
    total_real = n_real * blks * reps
    assert reps == len(ORDER)
    tile = 2 * n_gen

    blk, rep = lax.axis_index("blk"), lax.axis_index("rep")
    hi, lo = blk // GROUP, lax.rem(blk, GROUP)
    core, side = lax.rem(lo, 2), lo // 2
    sibling = (hi * GROUP + side * 2 + (1 - core), rep)
    across = (hi * GROUP + (1 - side) * 2 + core, rep)

    def z_partner(dz):
        return (blk, lax.rem(rep + dz, reps))

    def hi_partner(dh):
        return (lax.rem(hi + dh, his) * GROUP + lo, rep)

    half = n_real // 2
    c_gen, c_far = 2 * n_real, 3 * n_real

    def far_rows(m, forwarded):
        chunk, part = divmod(m, PIECES // 2)
        return pl.ds(c_far + chunk * n_real + (half if forwarded else 0) + part * piece, piece)

    def gen_rows(slot):
        return pl.ds(c_gen + slot * n_gen, n_gen)

    def block(dh, dz):
        return pl.ds(pl.multiple_of((dh * reps + ORDER.index(dz)) * n_gen, n_gen), n_gen)

    def remote(src, dst, send, recv, device):
        return pltpu.make_async_remote_copy(
            src_ref=src, dst_ref=dst, send_sem=send, recv_sem=recv, device_id=device, device_id_type=MESH
        )

    def z_copy(dz):
        back = reps - dz
        return remote(gen_ref, gen.at[block(0, back)], z_send.at[dz], z_recv.at[back], z_partner(dz))

    def hi_copy(dh, dz, src):
        back = his - dh
        return remote(src, gen.at[block(back, dz)], hi_send.at[dh, dz], hi_recv.at[back, dz], hi_partner(dh))

    def far_gen():
        return remote(gen_ref, oth.at[gen_rows(2)], far_send.at[0], far_recv.at[0], across)

    def far_real(m):
        return remote(
            oth.at[pl.ds(m * piece, piece)], oth.at[far_rows(m, False)],
            far_send.at[1 + m], far_recv.at[1 + m], across,
        )

    def sib_gen():
        return remote(gen_ref, oth.at[gen_rows(1)], sib_send.at[0], sib_recv.at[0], sibling)

    def sib_real():
        return remote(
            oth.at[pl.ds(0, n_real)], oth.at[pl.ds(n_real, n_real)], sib_send.at[1], sib_recv.at[1], sibling
        )

    def forward_gen():
        return remote(oth.at[gen_rows(2)], oth.at[gen_rows(3)], fwd_send.at[0], fwd_recv.at[0], sibling)

    def forward_real(m):
        return remote(
            oth.at[far_rows(m, False)], oth.at[far_rows(m, True)],
            fwd_send.at[1 + m], fwd_recv.at[1 + m], sibling,
        )

    def red_hi(dh, dz):
        back = his - dh
        return remote(
            acc.at[block(dh, dz)], from_hi.at[back, dz],
            red_hi_send.at[dh, dz], red_hi_recv.at[back, dz], hi_partner(dh),
        )

    def red_z(dz):
        back = reps - dz
        return remote(
            acc.at[block(0, dz)], from_z.at[back], red_z_send.at[dz], red_z_recv.at[back], z_partner(dz)
        )

    load_bank = pltpu.make_async_copy(bank_ref, bank, bank_sem)
    load_bank.start()
    partners = [sibling, across]
    partners += [z_partner(dz) for dz in range(1, reps)]
    partners += [hi_partner(dh) for dh in range(1, his)]
    barrier = pltpu.get_barrier_semaphore()
    for device in partners:
        pl.semaphore_signal(barrier, inc=1, device_id=device, device_id_type=MESH)
    load_bank.wait()

    def gather(i, carry):
        picked = [bank[pl.ds(rows_ref[i * 8 + k], 1), :] for k in range(8)]
        for k in range(8):
            p = i * 8 + k
            oth[pl.ds(p, 1), :] = picked[k]
        return carry

    lax.fori_loop(0, piece // 8, gather, 0)
    pl.semaphore_wait(barrier, len(partners))

    far_gen().start()
    z_copy(1).start()
    for dh in range(1, his):
        hi_copy(dh, 0, gen_ref).start()
    far_real(0).start()
    sib_gen().start()
    for m in range(1, PIECES):
        lax.fori_loop(m * piece // 8, (m + 1) * piece // 8, gather, 0)
        if m == 1:
            far_real(m).start()
    sib_real().start()

    def prepare_other(chunk):
        rows = pl.ds(chunk * n_real, n_real)
        value = oth[rows, :]
        high, low = split(value)
        oth_high[rows, :] = high
        oth_low[rows, :] = low
        norm = jnp.sum(value * value, axis=1, keepdims=True)
        oth_norm[chunk] = jnp.broadcast_to(norm, (n_real, 128)).T[0:8, :]

    def prepare_gen(q):
        rows = tile_rows(q)
        value = gen[rows, :]
        high, low = split(value)
        start = pl.multiple_of(2 * tile * q, tile)
        gen_both[pl.ds(start, tile), :] = high
        gen_both[pl.ds(pl.multiple_of(start + tile, tile), tile), :] = low
        gen_norm[rows, :] = jnp.sum(value * value, axis=1, keepdims=True)

    def tile_rows(q):
        return pl.ds(pl.multiple_of(q * tile, tile), tile)

    def add_pairs(q, chunk, scale):
        rows = tile_rows(q)
        others = pl.ds(pl.multiple_of(chunk * n_real, n_real), n_real)
        start = pl.multiple_of(2 * tile * q, tile)
        inner = product(
            gen_both[pl.ds(start, 2 * tile), :], gen_both[pl.ds(start, tile), :],
            oth_high[others, :], oth_low[others, :], ((1,), (1,)),
        )
        dist = jnp.maximum(gen_norm[rows, :] + oth_norm[chunk, 0:1, :] - 2.0 * inner, 0.0)
        wide = jnp.exp(dist * (-1.0 / (4.0 * width)))
        middle = wide * wide
        weight = (2.0 * (middle * middle) + middle + 0.5 * wide) * scale
        total[rows, :] += jnp.sum(weight, axis=1, keepdims=True)
        w_high, w_low = split(weight)
        w_both = jnp.concatenate([w_high, w_low], axis=0)
        step = 256
        for column in range(0, width, step):
            columns = pl.ds(column, step)
            acc[rows, columns] += product(
                w_both, w_high, oth_high[others, columns], oth_low[others, columns], ((1,), (0,))
            )

    self_scale, cross_scale = 1.0 / total_gen, -1.0 / total_real

    def take_far(m):
        far_real(m).wait_recv()
        forward_real(m).start()

    def take_z(dz):
        z_copy(reps - dz).wait_recv()
        for dh in range(1, his):
            hi_copy(dh, dz, gen.at[block(0, dz)]).start()

    def work(q, first, last):
        def chunk_pairs(chunk, carry):
            add_pairs(q, chunk, jnp.where(chunk == 2, self_scale, cross_scale))
            return carry

        lax.fori_loop(first, last, chunk_pairs, 0)

    def begin(q):
        prepare_gen(q)
        rows = tile_rows(q)
        acc[rows, :] = jnp.zeros((tile, width), jnp.float32)
        total[rows, :] = jnp.zeros((tile, 1), jnp.float32)

    def finish(q):
        rows = tile_rows(q)
        acc[rows, :] = total[rows, :] * gen[rows, :] - acc[rows, :]

    def loop(first, last, step):
        def body(i, carry):
            step(i)
            return carry

        lax.fori_loop(first, last, body, 0)

    gen[block(0, 0), :] = gen_ref[...]
    oth[gen_rows(0), :] = gen_ref[...]
    prepare_other(0)
    z_copy(1).wait_send()
    z_copy(3).start()
    take_z(1)
    sib_real().wait_recv()
    prepare_other(1)

    def stage_1(dh):
        @pl.when(dh >= 1)
        def _():
            for dz in ORDER[:2]:
                hi_copy(his - dh, dz, gen_ref).wait_recv()

        begin(2 * dh)
        work(2 * dh, 0, 2)

    loop(0, his, stage_1)
    z_copy(3).wait_send()
    z_copy(2).start()
    take_z(3)
    for m in range(2):
        far_real(m).wait_send()
    for m in range(2, PIECES):
        far_real(m).start()
    far_gen().wait_recv()
    forward_gen().start()
    for m in range(2):
        take_far(m)
    sib_gen().wait_recv()
    forward_gen().wait_recv()
    prepare_other(2)
    for m in range(2):
        forward_real(m).wait_recv()
    prepare_other(3)
    loop(0, his, lambda dh: work(2 * dh, 2, 4))
    take_z(2)
    begin(1)
    work(1, 0, 4)
    for m in range(2, PIECES):
        take_far(m)
    for m in range(2, PIECES):
        forward_real(m).wait_recv()
    prepare_other(4)

    def stage_3(dh):
        work(2 * dh, 4, 5)
        finish(2 * dh)
        red_hi(dh, 1).start()

    def stage_4(dh):
        for dz in ORDER[2:]:
            hi_copy(his - dh, dz, gen_ref).wait_recv()
        begin(2 * dh + 1)
        work(2 * dh + 1, 0, 5)
        finish(2 * dh + 1)

    def stage_5(q):
        work(q, 4, 5)
        finish(q)

    loop(1, his, stage_3)
    loop(1, his, stage_4)
    sends = (1, 2, 3, 0)
    for dh in range(1, his):
        red_hi(dh, 1).wait_send()
        red_hi(dh, 2).start()
    loop(0, 2, stage_5)

    for i, dz in enumerate(sends):
        for dh in range(1, his):
            red_hi(his - dh, dz).wait_recv()
            acc[block(0, dz), :] += from_hi[dh, dz]
        if dz > 0:
            red_z(dz).start()
        if i + 2 < len(sends):
            for dh in range(1, his):
                red_hi(dh, sends[i + 1]).wait_send()
                red_hi(dh, sends[i + 2]).start()
    result = acc[block(0, 0), :]
    for dz in sends[:-1]:
        red_z(reps - dz).wait_recv()
        result = result + from_z[dz]
    out_ref[...] = result

    sent = [far_gen(), sib_gen(), sib_real(), forward_gen(), z_copy(2)]
    sent += [far_real(m) for m in range(2, PIECES)] + [forward_real(m) for m in range(PIECES)]
    sent += [hi_copy(dh, dz, gen_ref) for dh in range(1, his) for dz in range(reps)]
    sent += [red_hi(dh, 0) for dh in range(1, his)] + [red_z(dz) for dz in range(1, reps)]
    for copy in sent:
        copy.wait_send()


def solution(mesh):
    blks, reps = mesh.shape["blk"], mesh.shape["rep"]
    his = blks // GROUP

    def on_device(generated, real_bank, subset_rows):
        n_gen, width = generated.shape
        n_real = subset_rows.shape[0]
        n_other = 5 * n_real
        n_rows = his * reps * n_gen
        dma = pltpu.SemaphoreType.DMA
        vmem = pl.BlockSpec(memory_space=pltpu.VMEM)
        pairs = n_rows * n_other
        return pl.pallas_call(
            functools.partial(kernel, (blks, reps)),
            out_shape=jax.ShapeDtypeStruct((n_gen, width), jnp.float32),
            in_specs=[pl.BlockSpec(memory_space=pltpu.SMEM), vmem, pl.BlockSpec(memory_space=pl.ANY)],
            out_specs=vmem,
            scratch_shapes=[
                pltpu.VMEM(real_bank.shape, jnp.float32),
                dma(()),
                pltpu.VMEM((n_other, width), jnp.float32),
                pltpu.VMEM((n_other, width), jnp.bfloat16),
                pltpu.VMEM((n_other, width), jnp.bfloat16),
                pltpu.VMEM((5, 8, n_real), jnp.float32),
                pltpu.VMEM((n_rows, width), jnp.float32),
                pltpu.VMEM((2 * n_rows, width), jnp.bfloat16),
                pltpu.VMEM((n_rows, 1), jnp.float32),
                pltpu.VMEM((n_rows, width), jnp.float32),
                pltpu.VMEM((n_rows, 1), jnp.float32),
                pltpu.VMEM((his, reps, n_gen, width), jnp.float32),
                pltpu.VMEM((reps, n_gen, width), jnp.float32),
                dma((2,)), dma((2,)),
                dma((1 + PIECES,)), dma((1 + PIECES,)),
                dma((1 + PIECES,)), dma((1 + PIECES,)),
                dma((reps,)), dma((reps,)),
                dma((his, reps)), dma((his, reps)),
                dma((his, reps)), dma((his, reps)),
                dma((reps,)), dma((reps,)),
            ],
            compiler_params=pltpu.CompilerParams(
                collective_id=0, has_side_effects=True, vmem_limit_bytes=60 * 1024 * 1024
            ),
            cost_estimate=pl.CostEstimate(
                flops=12 * pairs * width, bytes_accessed=4 * 1024 * width, transcendentals=pairs
            ),
        )(subset_rows, generated, real_bank)

    in_specs = (P(("blk", "rep"), None), P(("blk", "rep"), None), P(("blk", "rep")))
    return jax.shard_map(
        on_device, mesh=mesh, in_specs=in_specs, out_specs=P(("blk", "rep"), None), check_vma=False
    )
```

```python
import functools

import jax
import jax.numpy as jnp
from jax import lax
from jax.experimental import pallas as pl
from jax.experimental.pallas import tpu as pltpu
from jax.sharding import PartitionSpec as P

MESH = pl.DeviceIdType.MESH
GROUP = 4
ORDER = (0, 1, 3, 2)
PARTS = 2
PIECES = 4


def split(value):
    high = value.astype(jnp.bfloat16)
    return high, (value - high.astype(jnp.float32)).astype(jnp.bfloat16)


def dot(a, b, contract):
    return lax.dot_general(a, b, (contract, ((), ())), preferred_element_type=jnp.float32)


def product(a_both, a_high, b_high, b_low, contract):
    rows = a_high.shape[0]
    both = dot(a_both, b_high, contract)
    return both[:rows] + (both[rows:] + dot(a_high, b_low, contract))


def kernel(
    sizes,
    rows_ref, gen_ref, bank_ref, out_ref, bank, bank_sem,
    oth, oth_high, oth_low, oth_norm,
    gen, gen_both, gen_norm, acc, total, from_hi, from_z,
    sib_send, sib_recv, far_send, far_recv, fwd_send, fwd_recv,
    z_send, z_recv, hi_send, hi_recv, red_hi_send, red_hi_recv, red_z_send, red_z_recv,
):
    blks, reps = sizes
    his = blks // GROUP
    n_gen, width = gen_ref.shape
    n_real = rows_ref.shape[0]
    piece = n_real // PIECES
    total_gen = n_gen * blks * reps
    total_real = n_real * blks * reps
    assert reps == len(ORDER)
    tile = 2 * n_gen

    blk, rep = lax.axis_index("blk"), lax.axis_index("rep")
    hi, lo = blk // GROUP, lax.rem(blk, GROUP)
    core, side = lax.rem(lo, 2), lo // 2
    sibling = (hi * GROUP + side * 2 + (1 - core), rep)
    across = (hi * GROUP + (1 - side) * 2 + core, rep)

    def z_partner(dz):
        return (blk, lax.rem(rep + dz, reps))

    def hi_partner(dh):
        return (lax.rem(hi + dh, his) * GROUP + lo, rep)

    half = n_real // 2
    c_gen, c_far = 2 * n_real, 3 * n_real

    def far_rows(m, forwarded):
        chunk, part = divmod(m, PIECES // 2)
        return pl.ds(c_far + chunk * n_real + (half if forwarded else 0) + part * piece, piece)

    def gen_rows(slot):
        return pl.ds(c_gen + slot * n_gen, n_gen)

    def block(dh, dz):
        return pl.ds(pl.multiple_of((dh * reps + ORDER.index(dz)) * n_gen, n_gen), n_gen)

    def remote(src, dst, send, recv, device):
        return pltpu.make_async_remote_copy(
            src_ref=src, dst_ref=dst, send_sem=send, recv_sem=recv, device_id=device, device_id_type=MESH
        )

    def z_copy(dz):
        back = reps - dz
        return remote(gen_ref, gen.at[block(0, back)], z_send.at[dz], z_recv.at[back], z_partner(dz))

    def hi_copy(dh, dz, src):
        back = his - dh
        return remote(src, gen.at[block(back, dz)], hi_send.at[dh, dz], hi_recv.at[back, dz], hi_partner(dh))

    def far_gen():
        return remote(gen_ref, oth.at[gen_rows(2)], far_send.at[0], far_recv.at[0], across)

    def far_real(m):
        return remote(
            oth.at[pl.ds(m * piece, piece)], oth.at[far_rows(m, False)],
            far_send.at[1 + m], far_recv.at[1 + m], across,
        )

    def sib_gen():
        return remote(gen_ref, oth.at[gen_rows(1)], sib_send.at[0], sib_recv.at[0], sibling)

    def sib_real():
        return remote(
            oth.at[pl.ds(0, n_real)], oth.at[pl.ds(n_real, n_real)], sib_send.at[1], sib_recv.at[1], sibling
        )

    def forward_gen():
        return remote(oth.at[gen_rows(2)], oth.at[gen_rows(3)], fwd_send.at[0], fwd_recv.at[0], sibling)

    def forward_real(m):
        return remote(
            oth.at[far_rows(m, False)], oth.at[far_rows(m, True)],
            fwd_send.at[1 + m], fwd_recv.at[1 + m], sibling,
        )

    n_part = n_gen // PARTS

    def part_of(dh, dz, p):
        start = (dh * reps + ORDER.index(dz)) * n_gen + p * n_part
        return pl.ds(pl.multiple_of(start, n_part), n_part)

    def red_hi(dh, dz, p):
        back = his - dh
        return remote(
            acc.at[part_of(dh, dz, p)], from_hi.at[back, dz, pl.ds(p * n_part, n_part)],
            red_hi_send.at[dh, dz, p], red_hi_recv.at[back, dz, p], hi_partner(dh),
        )

    def red_z(dz, p):
        back = reps - dz
        return remote(
            acc.at[part_of(0, dz, p)], from_z.at[back, pl.ds(p * n_part, n_part)],
            red_z_send.at[dz, p], red_z_recv.at[back, p], z_partner(dz),
        )

    load_bank = pltpu.make_async_copy(bank_ref, bank, bank_sem)
    load_bank.start()
    partners = [sibling, across]
    partners += [z_partner(dz) for dz in range(1, reps)]
    partners += [hi_partner(dh) for dh in range(1, his)]
    barrier = pltpu.get_barrier_semaphore()
    for device in partners:
        pl.semaphore_signal(barrier, inc=1, device_id=device, device_id_type=MESH)
    load_bank.wait()

    def gather(i, carry):
        picked = [bank[pl.ds(rows_ref[i * 8 + k], 1), :] for k in range(8)]
        for k in range(8):
            p = i * 8 + k
            oth[pl.ds(p, 1), :] = picked[k]
        return carry

    lax.fori_loop(0, piece // 8, gather, 0)
    pl.semaphore_wait(barrier, len(partners))

    far_gen().start()
    z_copy(1).start()
    for dh in range(1, his):
        hi_copy(dh, 0, gen_ref).start()
    far_real(0).start()
    sib_gen().start()
    for m in range(1, PIECES):
        lax.fori_loop(m * piece // 8, (m + 1) * piece // 8, gather, 0)
        if m == 1:
            far_real(m).start()
    sib_real().start()

    def prepare_half(chunk, which):
        rows = pl.ds(chunk * n_real + which * half, half)
        value = oth[rows, :]
        high, low = split(value)
        oth_high[rows, :] = high
        oth_low[rows, :] = low
        norm = jnp.sum(value * value, axis=1, keepdims=True)
        oth_norm[chunk, :, which * half : (which + 1) * half] = jnp.broadcast_to(norm, (half, 128)).T[0:8, :]

    def prepare_other(chunk):
        prepare_half(chunk, 0)
        prepare_half(chunk, 1)

    def prepare_gen(q):
        rows = tile_rows(q)
        value = gen[rows, :]
        high, low = split(value)
        start = pl.multiple_of(2 * tile * q, tile)
        gen_both[pl.ds(start, tile), :] = high
        gen_both[pl.ds(pl.multiple_of(start + tile, tile), tile), :] = low
        gen_norm[rows, :] = jnp.sum(value * value, axis=1, keepdims=True)

    def tile_rows(q):
        return pl.ds(pl.multiple_of(q * tile, tile), tile)

    def add_pairs(q, chunk, scale):
        rows = tile_rows(q)
        others = pl.ds(pl.multiple_of(chunk * n_real, n_real), n_real)
        start = pl.multiple_of(2 * tile * q, tile)
        inner = product(
            gen_both[pl.ds(start, 2 * tile), :], gen_both[pl.ds(start, tile), :],
            oth_high[others, :], oth_low[others, :], ((1,), (1,)),
        )
        dist = jnp.maximum(gen_norm[rows, :] + oth_norm[chunk, 0:1, :] - 2.0 * inner, 0.0)
        wide = jnp.exp(dist * (-1.0 / (4.0 * width)))
        middle = wide * wide
        weight = (2.0 * (middle * middle) + middle + 0.5 * wide) * scale
        total[rows, :] += jnp.sum(weight, axis=1, keepdims=True)
        w_high, w_low = split(weight)
        w_both = jnp.concatenate([w_high, w_low], axis=0)
        step = 256
        for column in range(0, width, step):
            columns = pl.ds(column, step)
            acc[rows, columns] += product(
                w_both, w_high, oth_high[others, columns], oth_low[others, columns], ((1,), (0,))
            )

    self_scale, cross_scale = 1.0 / total_gen, -1.0 / total_real

    def take_far(m):
        far_real(m).wait_recv()
        forward_real(m).start()

    def take_z(dz):
        z_copy(reps - dz).wait_recv()
        for dh in range(1, his):
            hi_copy(dh, dz, gen.at[block(0, dz)]).start()

    def work(q, first, last):
        def chunk_pairs(chunk, carry):
            add_pairs(q, chunk, jnp.where(chunk == 2, self_scale, cross_scale))
            return carry

        lax.fori_loop(first, last, chunk_pairs, 0)

    def begin(q):
        prepare_gen(q)
        rows = tile_rows(q)
        acc[rows, :] = jnp.zeros((tile, width), jnp.float32)
        total[rows, :] = jnp.zeros((tile, 1), jnp.float32)

    def finish(q):
        rows = tile_rows(q)
        acc[rows, :] = total[rows, :] * gen[rows, :] - acc[rows, :]

    def loop(first, last, step):
        def body(i, carry):
            step(i)
            return carry

        lax.fori_loop(first, last, body, 0)

    gen[block(0, 0), :] = gen_ref[...]
    oth[gen_rows(0), :] = gen_ref[...]
    prepare_other(0)
    z_copy(1).wait_send()
    z_copy(3).start()
    take_z(1)
    far_real(2).start()
    sib_real().wait_recv()
    prepare_other(1)

    def stage_1(dh):
        @pl.when(dh >= 1)
        def _():
            for dz in ORDER[:2]:
                hi_copy(his - dh, dz, gen_ref).wait_recv()

        begin(2 * dh)
        work(2 * dh, 0, 2)

    loop(0, his, stage_1)
    z_copy(3).wait_send()
    z_copy(2).start()
    take_z(3)
    far_real(3).start()
    far_gen().wait_recv()
    forward_gen().start()
    for m in range(2):
        take_far(m)
    sib_gen().wait_recv()
    forward_gen().wait_recv()
    prepare_other(2)
    for m in range(2):
        forward_real(m).wait_recv()
    prepare_other(3)
    loop(0, his, lambda dh: work(2 * dh, 2, 4))
    take_z(2)
    begin(1)
    work(1, 0, 4)
    for m in range(2, PIECES):
        take_far(m)
    prepare_half(4, 0)
    for m in range(2, PIECES):
        forward_real(m).wait_recv()
    prepare_half(4, 1)

    def stage_3(dh):
        work(2 * dh, 4, 5)
        finish(2 * dh)
        for p in range(PARTS):
            red_hi(dh, 1, p).start()

    def stage_4(dh):
        for dz in ORDER[2:]:
            hi_copy(his - dh, dz, gen_ref).wait_recv()
        begin(2 * dh + 1)
        work(2 * dh + 1, 0, 5)
        finish(2 * dh + 1)

    def stage_5(q):
        work(q, 4, 5)
        finish(q)

    loop(1, his, stage_3)
    loop(1, his, stage_4)
    sends = [(dz, p) for dz in (1, 2, 3, 0) for p in range(PARTS)]

    def next_send(i):
        for dh in range(1, his):
            red_hi(dh, *sends[i]).wait_send()
            red_hi(dh, *sends[i + 2]).start()

    next_send(0)
    next_send(1)
    loop(0, 2, stage_5)

    for i, (dz, p) in enumerate(sends):
        rows = part_of(0, dz, p)
        value = acc[rows, :]
        for dh in range(1, his):
            red_hi(his - dh, dz, p).wait_recv()
            value = value + from_hi[dh, dz, pl.ds(p * n_part, n_part), :]
        acc[rows, :] = value
        if dz > 0:
            red_z(dz, p).start()
        if i + 4 < len(sends):
            next_send(i + 2)
    for p in range(PARTS):
        result = acc[part_of(0, 0, p), :]
        for dz in (1, 2, 3):
            red_z(reps - dz, p).wait_recv()
            result = result + from_z[dz, pl.ds(p * n_part, n_part), :]
        out_ref[pl.ds(p * n_part, n_part), :] = result

    sent = [far_gen(), sib_gen(), sib_real(), forward_gen(), z_copy(2)]
    sent += [far_real(m) for m in range(PIECES)] + [forward_real(m) for m in range(PIECES)]
    sent += [hi_copy(dh, dz, gen_ref) for dh in range(1, his) for dz in range(reps)]
    sent += [red_hi(dh, 0, p) for dh in range(1, his) for p in range(PARTS)]
    sent += [red_z(dz, p) for dz in range(1, reps) for p in range(PARTS)]
    for copy in sent:
        copy.wait_send()


def solution(mesh):
    blks, reps = mesh.shape["blk"], mesh.shape["rep"]
    his = blks // GROUP

    def on_device(generated, real_bank, subset_rows):
        n_gen, width = generated.shape
        n_real = subset_rows.shape[0]
        n_other = 5 * n_real
        n_rows = his * reps * n_gen
        dma = pltpu.SemaphoreType.DMA
        vmem = pl.BlockSpec(memory_space=pltpu.VMEM)
        pairs = n_rows * n_other
        return pl.pallas_call(
            functools.partial(kernel, (blks, reps)),
            out_shape=jax.ShapeDtypeStruct((n_gen, width), jnp.float32),
            in_specs=[pl.BlockSpec(memory_space=pltpu.SMEM), vmem, pl.BlockSpec(memory_space=pl.ANY)],
            out_specs=vmem,
            scratch_shapes=[
                pltpu.VMEM(real_bank.shape, jnp.float32),
                dma(()),
                pltpu.VMEM((n_other, width), jnp.float32),
                pltpu.VMEM((n_other, width), jnp.bfloat16),
                pltpu.VMEM((n_other, width), jnp.bfloat16),
                pltpu.VMEM((5, 8, n_real), jnp.float32),
                pltpu.VMEM((n_rows, width), jnp.float32),
                pltpu.VMEM((2 * n_rows, width), jnp.bfloat16),
                pltpu.VMEM((n_rows, 1), jnp.float32),
                pltpu.VMEM((n_rows, width), jnp.float32),
                pltpu.VMEM((n_rows, 1), jnp.float32),
                pltpu.VMEM((his, reps, n_gen, width), jnp.float32),
                pltpu.VMEM((reps, n_gen, width), jnp.float32),
                dma((2,)), dma((2,)),
                dma((1 + PIECES,)), dma((1 + PIECES,)),
                dma((1 + PIECES,)), dma((1 + PIECES,)),
                dma((reps,)), dma((reps,)),
                dma((his, reps)), dma((his, reps)),
                dma((his, reps, PARTS)), dma((his, reps, PARTS)),
                dma((reps, PARTS)), dma((reps, PARTS)),
            ],
            compiler_params=pltpu.CompilerParams(
                collective_id=0, has_side_effects=True, vmem_limit_bytes=60 * 1024 * 1024
            ),
            cost_estimate=pl.CostEstimate(
                flops=12 * pairs * width, bytes_accessed=4 * 1024 * width, transcendentals=pairs
            ),
        )(subset_rows, generated, real_bank)

    in_specs = (P(("blk", "rep"), None), P(("blk", "rep"), None), P(("blk", "rep")))
    return jax.shard_map(
        on_device, mesh=mesh, in_specs=in_specs, out_specs=P(("blk", "rep"), None), check_vma=False
    )
```

```python
import functools

import jax
import jax.numpy as jnp
from jax import lax
from jax.experimental import pallas as pl
from jax.experimental.pallas import tpu as pltpu
from jax.sharding import PartitionSpec as P

MESH = pl.DeviceIdType.MESH
GROUP = 4
ORDER = (0, 1, 3, 2)
PARTS = 2
PIECES = 4


def split(value):
    high = value.astype(jnp.bfloat16)
    return high, (value - high.astype(jnp.float32)).astype(jnp.bfloat16)


def dot(a, b, contract):
    return lax.dot_general(a, b, (contract, ((), ())), preferred_element_type=jnp.float32)


def product(a_both, a_high, b_high, b_low, contract):
    rows = a_high.shape[0]
    both = dot(a_both, b_high, contract)
    return both[:rows] + (both[rows:] + dot(a_high, b_low, contract))


def kernel(
    sizes,
    gen_ref, real_ref, out_ref,
    oth, oth_high, oth_low, oth_norm,
    gen, gen_both, gen_norm, acc, total, from_hi, from_z,
    sib_send, sib_recv, far_send, far_recv, fwd_send, fwd_recv,
    z_send, z_recv, hi_send, hi_recv, red_hi_send, red_hi_recv, red_z_send, red_z_recv,
):
    blks, reps = sizes
    his = blks // GROUP
    n_gen, width = gen_ref.shape
    n_real = real_ref.shape[0]
    piece = n_real // PIECES
    total_gen = n_gen * blks * reps
    total_real = n_real * blks * reps
    assert reps == len(ORDER)
    tile = 2 * n_gen

    blk, rep = lax.axis_index("blk"), lax.axis_index("rep")
    hi, lo = blk // GROUP, lax.rem(blk, GROUP)
    core, side = lax.rem(lo, 2), lo // 2
    sibling = (hi * GROUP + side * 2 + (1 - core), rep)
    across = (hi * GROUP + (1 - side) * 2 + core, rep)

    def z_partner(dz):
        return (blk, lax.rem(rep + dz, reps))

    def hi_partner(dh):
        return (lax.rem(hi + dh, his) * GROUP + lo, rep)

    half = n_real // 2
    c_gen, c_far = 2 * n_real, 3 * n_real

    def far_rows(m, forwarded):
        chunk, part = divmod(m, PIECES // 2)
        return pl.ds(c_far + chunk * n_real + (half if forwarded else 0) + part * piece, piece)

    def gen_rows(slot):
        return pl.ds(c_gen + slot * n_gen, n_gen)

    def block(dh, dz):
        return pl.ds(pl.multiple_of((dh * reps + ORDER.index(dz)) * n_gen, n_gen), n_gen)

    def remote(src, dst, send, recv, device):
        return pltpu.make_async_remote_copy(
            src_ref=src, dst_ref=dst, send_sem=send, recv_sem=recv, device_id=device, device_id_type=MESH
        )

    def z_copy(dz):
        back = reps - dz
        return remote(gen_ref, gen.at[block(0, back)], z_send.at[dz], z_recv.at[back], z_partner(dz))

    def hi_copy(dh, dz, src):
        back = his - dh
        return remote(src, gen.at[block(back, dz)], hi_send.at[dh, dz], hi_recv.at[back, dz], hi_partner(dh))

    def far_gen():
        return remote(gen_ref, oth.at[gen_rows(2)], far_send.at[0], far_recv.at[0], across)

    def far_real(m):
        return remote(
            real_ref.at[pl.ds(m * piece, piece)], oth.at[far_rows(m, False)],
            far_send.at[1 + m], far_recv.at[1 + m], across,
        )

    def sib_gen():
        return remote(gen_ref, oth.at[gen_rows(1)], sib_send.at[0], sib_recv.at[0], sibling)

    def sib_real():
        return remote(
            real_ref, oth.at[pl.ds(n_real, n_real)], sib_send.at[1], sib_recv.at[1], sibling
        )

    def forward_gen():
        return remote(oth.at[gen_rows(2)], oth.at[gen_rows(3)], fwd_send.at[0], fwd_recv.at[0], sibling)

    def forward_real(m):
        return remote(
            oth.at[far_rows(m, False)], oth.at[far_rows(m, True)],
            fwd_send.at[1 + m], fwd_recv.at[1 + m], sibling,
        )

    n_part = n_gen // PARTS

    def part_of(dh, dz, p):
        start = (dh * reps + ORDER.index(dz)) * n_gen + p * n_part
        return pl.ds(pl.multiple_of(start, n_part), n_part)

    def red_hi(dh, dz, p):
        back = his - dh
        return remote(
            acc.at[part_of(dh, dz, p)], from_hi.at[back, dz, pl.ds(p * n_part, n_part)],
            red_hi_send.at[dh, dz, p], red_hi_recv.at[back, dz, p], hi_partner(dh),
        )

    def red_z(dz, p):
        back = reps - dz
        return remote(
            acc.at[part_of(0, dz, p)], from_z.at[back, pl.ds(p * n_part, n_part)],
            red_z_send.at[dz, p], red_z_recv.at[back, p], z_partner(dz),
        )

    partners = [sibling, across]
    partners += [z_partner(dz) for dz in range(1, reps)]
    partners += [hi_partner(dh) for dh in range(1, his)]
    barrier = pltpu.get_barrier_semaphore()
    for device in partners:
        pl.semaphore_signal(barrier, inc=1, device_id=device, device_id_type=MESH)
    pl.semaphore_wait(barrier, len(partners))

    far_gen().start()
    z_copy(1).start()
    for dh in range(1, his):
        hi_copy(dh, 0, gen_ref).start()
    far_real(0).start()
    sib_gen().start()
    far_real(1).start()
    sib_real().start()

    def prepare_half(chunk, which):
        rows = pl.ds(chunk * n_real + which * half, half)
        value = real_ref[rows, :] if chunk == 0 else oth[rows, :]
        high, low = split(value)
        oth_high[rows, :] = high
        oth_low[rows, :] = low
        norm = jnp.sum(value * value, axis=1, keepdims=True)
        oth_norm[chunk, :, which * half : (which + 1) * half] = jnp.broadcast_to(norm, (half, 128)).T[0:8, :]

    def prepare_other(chunk):
        prepare_half(chunk, 0)
        prepare_half(chunk, 1)

    def prepare_gen(q):
        rows = tile_rows(q)
        value = gen[rows, :]
        high, low = split(value)
        start = pl.multiple_of(2 * tile * q, tile)
        gen_both[pl.ds(start, tile), :] = high
        gen_both[pl.ds(pl.multiple_of(start + tile, tile), tile), :] = low
        gen_norm[rows, :] = jnp.sum(value * value, axis=1, keepdims=True)

    def tile_rows(q):
        return pl.ds(pl.multiple_of(q * tile, tile), tile)

    def add_pairs(q, chunk, scale):
        rows = tile_rows(q)
        others = pl.ds(pl.multiple_of(chunk * n_real, n_real), n_real)
        start = pl.multiple_of(2 * tile * q, tile)
        inner = product(
            gen_both[pl.ds(start, 2 * tile), :], gen_both[pl.ds(start, tile), :],
            oth_high[others, :], oth_low[others, :], ((1,), (1,)),
        )
        dist = jnp.maximum(gen_norm[rows, :] + oth_norm[chunk, 0:1, :] - 2.0 * inner, 0.0)
        wide = jnp.exp(dist * (-1.0 / (4.0 * width)))
        middle = wide * wide
        weight = (2.0 * (middle * middle) + middle + 0.5 * wide) * scale
        total[rows, :] += jnp.sum(weight, axis=1, keepdims=True)
        w_high, w_low = split(weight)
        w_both = jnp.concatenate([w_high, w_low], axis=0)
        step = 256
        for column in range(0, width, step):
            columns = pl.ds(column, step)
            acc[rows, columns] += product(
                w_both, w_high, oth_high[others, columns], oth_low[others, columns], ((1,), (0,))
            )

    self_scale, cross_scale = 1.0 / total_gen, -1.0 / total_real

    def take_far(m):
        far_real(m).wait_recv()
        forward_real(m).start()

    def take_z(dz):
        z_copy(reps - dz).wait_recv()
        for dh in range(1, his):
            hi_copy(dh, dz, gen.at[block(0, dz)]).start()

    def work(q, first, last):
        def chunk_pairs(chunk, carry):
            add_pairs(q, chunk, jnp.where(chunk == 2, self_scale, cross_scale))
            return carry

        lax.fori_loop(first, last, chunk_pairs, 0)

    def begin(q):
        prepare_gen(q)
        rows = tile_rows(q)
        acc[rows, :] = jnp.zeros((tile, width), jnp.float32)
        total[rows, :] = jnp.zeros((tile, 1), jnp.float32)

    def finish(q):
        rows = tile_rows(q)
        acc[rows, :] = total[rows, :] * gen[rows, :] - acc[rows, :]

    def loop(first, last, step):
        def body(i, carry):
            step(i)
            return carry

        lax.fori_loop(first, last, body, 0)

    gen[block(0, 0), :] = gen_ref[...]
    oth[gen_rows(0), :] = gen_ref[...]
    prepare_other(0)
    z_copy(1).wait_send()
    z_copy(3).start()
    take_z(1)
    far_real(2).start()
    sib_real().wait_recv()
    prepare_other(1)

    def stage_1(dh):
        @pl.when(dh >= 1)
        def _():
            for dz in ORDER[:2]:
                hi_copy(his - dh, dz, gen_ref).wait_recv()

        begin(2 * dh)
        work(2 * dh, 0, 2)

    loop(0, his, stage_1)
    z_copy(3).wait_send()
    z_copy(2).start()
    take_z(3)
    far_real(3).start()
    far_gen().wait_recv()
    forward_gen().start()
    for m in range(2):
        take_far(m)
    sib_gen().wait_recv()
    forward_gen().wait_recv()
    prepare_other(2)
    for m in range(2):
        forward_real(m).wait_recv()
    prepare_other(3)
    loop(0, his, lambda dh: work(2 * dh, 2, 4))
    take_z(2)
    begin(1)
    work(1, 0, 4)
    for m in range(2, PIECES):
        take_far(m)
    prepare_half(4, 0)
    for m in range(2, PIECES):
        forward_real(m).wait_recv()
    prepare_half(4, 1)

    def stage_3(dh):
        work(2 * dh, 4, 5)
        finish(2 * dh)
        for p in range(PARTS):
            red_hi(dh, 1, p).start()

    def stage_4(dh):
        for dz in ORDER[2:]:
            hi_copy(his - dh, dz, gen_ref).wait_recv()
        begin(2 * dh + 1)
        work(2 * dh + 1, 0, 5)
        finish(2 * dh + 1)

    def stage_5(q):
        work(q, 4, 5)
        finish(q)

    loop(1, his, stage_3)
    loop(1, his, stage_4)
    sends = [(dz, p) for dz in (1, 2, 3, 0) for p in range(PARTS)]

    def next_send(i):
        for dh in range(1, his):
            red_hi(dh, *sends[i]).wait_send()
            red_hi(dh, *sends[i + 2]).start()

    next_send(0)
    next_send(1)
    loop(0, 2, stage_5)

    for i, (dz, p) in enumerate(sends):
        rows = part_of(0, dz, p)
        value = acc[rows, :]
        for dh in range(1, his):
            red_hi(his - dh, dz, p).wait_recv()
            value = value + from_hi[dh, dz, pl.ds(p * n_part, n_part), :]
        acc[rows, :] = value
        if dz > 0:
            red_z(dz, p).start()
        if i + 4 < len(sends):
            next_send(i + 2)
    for p in range(PARTS):
        result = acc[part_of(0, 0, p), :]
        for dz in (1, 2, 3):
            red_z(reps - dz, p).wait_recv()
            result = result + from_z[dz, pl.ds(p * n_part, n_part), :]
        out_ref[pl.ds(p * n_part, n_part), :] = result

    sent = [far_gen(), sib_gen(), sib_real(), forward_gen(), z_copy(2)]
    sent += [far_real(m) for m in range(PIECES)] + [forward_real(m) for m in range(PIECES)]
    sent += [hi_copy(dh, dz, gen_ref) for dh in range(1, his) for dz in range(reps)]
    sent += [red_hi(dh, 0, p) for dh in range(1, his) for p in range(PARTS)]
    sent += [red_z(dz, p) for dz in range(1, reps) for p in range(PARTS)]
    for copy in sent:
        copy.wait_send()


def solution(mesh):
    blks, reps = mesh.shape["blk"], mesh.shape["rep"]
    his = blks // GROUP

    def on_device(generated, real_bank, subset_rows):
        n_gen, width = generated.shape
        n_real = subset_rows.shape[0]
        n_other = 5 * n_real
        n_rows = his * reps * n_gen
        dma = pltpu.SemaphoreType.DMA
        vmem = pl.BlockSpec(memory_space=pltpu.VMEM)
        pairs = n_rows * n_other
        return pl.pallas_call(
            functools.partial(kernel, (blks, reps)),
            out_shape=jax.ShapeDtypeStruct((n_gen, width), jnp.float32),
            in_specs=[vmem, vmem],
            out_specs=vmem,
            scratch_shapes=[
                pltpu.VMEM((n_other, width), jnp.float32),
                pltpu.VMEM((n_other, width), jnp.bfloat16),
                pltpu.VMEM((n_other, width), jnp.bfloat16),
                pltpu.VMEM((5, 8, n_real), jnp.float32),
                pltpu.VMEM((n_rows, width), jnp.float32),
                pltpu.VMEM((2 * n_rows, width), jnp.bfloat16),
                pltpu.VMEM((n_rows, 1), jnp.float32),
                pltpu.VMEM((n_rows, width), jnp.float32),
                pltpu.VMEM((n_rows, 1), jnp.float32),
                pltpu.VMEM((his, reps, n_gen, width), jnp.float32),
                pltpu.VMEM((reps, n_gen, width), jnp.float32),
                dma((2,)), dma((2,)),
                dma((1 + PIECES,)), dma((1 + PIECES,)),
                dma((1 + PIECES,)), dma((1 + PIECES,)),
                dma((reps,)), dma((reps,)),
                dma((his, reps)), dma((his, reps)),
                dma((his, reps, PARTS)), dma((his, reps, PARTS)),
                dma((reps, PARTS)), dma((reps, PARTS)),
            ],
            compiler_params=pltpu.CompilerParams(
                collective_id=0, has_side_effects=True, vmem_limit_bytes=60 * 1024 * 1024
            ),
            cost_estimate=pl.CostEstimate(
                flops=12 * pairs * width, bytes_accessed=4 * 1024 * width, transcendentals=pairs
            ),
        )(generated, real_bank.at[subset_rows].get(mode="promise_in_bounds", wrap_negative_indices=False))

    in_specs = (P(("blk", "rep"), None), P(("blk", "rep"), None), P(("blk", "rep")))
    return jax.shard_map(
        on_device, mesh=mesh, in_specs=in_specs, out_specs=P(("blk", "rep"), None), check_vma=False
    )
```

```python
import functools

import jax
import jax.numpy as jnp
from jax import lax
from jax.experimental import pallas as pl
from jax.experimental.pallas import tpu as pltpu
from jax.sharding import PartitionSpec as P

MESH = pl.DeviceIdType.MESH
GROUP = 4
ORDER = (0, 1, 3, 2)
PARTS = 2
PIECES = 4


def split(value):
    high = value.astype(jnp.bfloat16)
    return high, (value - high.astype(jnp.float32)).astype(jnp.bfloat16)


def dot(a, b, contract):
    return lax.dot_general(a, b, (contract, ((), ())), preferred_element_type=jnp.float32)


def product(a_both, a_high, b_high, b_low, contract):
    rows = a_high.shape[0]
    both = dot(a_both, b_high, contract)
    return both[:rows] + (both[rows:] + dot(a_high, b_low, contract))


def kernel(
    sizes,
    rows_ref, gen_ref, bank_ref, out_ref, bank, load_sem,
    oth, oth_high, oth_low, oth_norm,
    gen, gen_both, gen_norm, acc, total, from_hi, from_z,
    sib_send, sib_recv, far_send, far_recv, fwd_send, fwd_recv,
    z_send, z_recv, hi_send, hi_recv, red_hi_send, red_hi_recv, red_z_send, red_z_recv,
):
    blks, reps = sizes
    his = blks // GROUP
    n_gen, width = gen_ref.shape
    n_real = rows_ref.shape[0]
    piece = n_real // PIECES
    total_gen = n_gen * blks * reps
    total_real = n_real * blks * reps
    assert reps == len(ORDER)
    tile = 2 * n_gen

    blk, rep = lax.axis_index("blk"), lax.axis_index("rep")
    hi, lo = blk // GROUP, lax.rem(blk, GROUP)
    core, side = lax.rem(lo, 2), lo // 2
    sibling = (hi * GROUP + side * 2 + (1 - core), rep)
    across = (hi * GROUP + (1 - side) * 2 + core, rep)

    def z_partner(dz):
        return (blk, lax.rem(rep + dz, reps))

    def hi_partner(dh):
        return (lax.rem(hi + dh, his) * GROUP + lo, rep)

    half = n_real // 2
    c_gen, c_far = 2 * n_real, 3 * n_real

    def far_rows(m, forwarded):
        chunk, part = divmod(m, PIECES // 2)
        return pl.ds(c_far + chunk * n_real + (half if forwarded else 0) + part * piece, piece)

    def gen_rows(slot):
        return pl.ds(c_gen + slot * n_gen, n_gen)

    def block(dh, dz):
        return pl.ds(pl.multiple_of((dh * reps + ORDER.index(dz)) * n_gen, n_gen), n_gen)

    own = gen.at[block(0, 0)]

    def remote(src, dst, send, recv, device):
        return pltpu.make_async_remote_copy(
            src_ref=src, dst_ref=dst, send_sem=send, recv_sem=recv, device_id=device, device_id_type=MESH
        )

    def z_copy(dz):
        back = reps - dz
        return remote(own, gen.at[block(0, back)], z_send.at[dz], z_recv.at[back], z_partner(dz))

    def hi_copy(dh, dz, src):
        back = his - dh
        return remote(src, gen.at[block(back, dz)], hi_send.at[dh, dz], hi_recv.at[back, dz], hi_partner(dh))

    def far_gen():
        return remote(own, oth.at[gen_rows(2)], far_send.at[0], far_recv.at[0], across)

    def far_real(m):
        return remote(
            oth.at[pl.ds(m * piece, piece)], oth.at[far_rows(m, False)],
            far_send.at[1 + m], far_recv.at[1 + m], across,
        )

    def sib_gen():
        return remote(own, oth.at[gen_rows(1)], sib_send.at[0], sib_recv.at[0], sibling)

    def sib_real():
        return remote(
            oth.at[pl.ds(0, n_real)], oth.at[pl.ds(n_real, n_real)], sib_send.at[1], sib_recv.at[1], sibling
        )

    def forward_gen():
        return remote(oth.at[gen_rows(2)], oth.at[gen_rows(3)], fwd_send.at[0], fwd_recv.at[0], sibling)

    def forward_real(m):
        return remote(
            oth.at[far_rows(m, False)], oth.at[far_rows(m, True)],
            fwd_send.at[1 + m], fwd_recv.at[1 + m], sibling,
        )

    n_part = n_gen // PARTS

    def part_of(dh, dz, p):
        start = (dh * reps + ORDER.index(dz)) * n_gen + p * n_part
        return pl.ds(pl.multiple_of(start, n_part), n_part)

    def red_hi(dh, dz, p):
        back = his - dh
        return remote(
            acc.at[part_of(dh, dz, p)], from_hi.at[back, dz, pl.ds(p * n_part, n_part)],
            red_hi_send.at[dh, dz, p], red_hi_recv.at[back, dz, p], hi_partner(dh),
        )

    def red_z(dz, p):
        back = reps - dz
        return remote(
            acc.at[part_of(0, dz, p)], from_z.at[back, pl.ds(p * n_part, n_part)],
            red_z_send.at[dz, p], red_z_recv.at[back, p], z_partner(dz),
        )

    loads = [
        pltpu.make_async_copy(bank_ref, bank, load_sem.at[0]),
        pltpu.make_async_copy(gen_ref, own, load_sem.at[1]),
        pltpu.make_async_copy(gen_ref, oth.at[gen_rows(0)], load_sem.at[2]),
    ]
    for load in loads:
        load.start()
    partners = [sibling, across]
    partners += [z_partner(dz) for dz in range(1, reps)]
    partners += [hi_partner(dh) for dh in range(1, his)]
    barrier = pltpu.get_barrier_semaphore()
    for device in partners:
        pl.semaphore_signal(barrier, inc=1, device_id=device, device_id_type=MESH)
    for load in loads:
        load.wait()

    def gather(i, carry):
        picked = [bank[pl.ds(rows_ref[i * 8 + k], 1), :] for k in range(8)]
        for k in range(8):
            p = i * 8 + k
            oth[pl.ds(p, 1), :] = picked[k]
        return carry

    lax.fori_loop(0, piece // 8, gather, 0)
    pl.semaphore_wait(barrier, len(partners))

    far_gen().start()
    z_copy(1).start()
    for dh in range(1, his):
        hi_copy(dh, 0, own).start()
    far_real(0).start()
    sib_gen().start()
    for m in range(1, PIECES):
        lax.fori_loop(m * piece // 8, (m + 1) * piece // 8, gather, 0)
        if m == 1:
            far_real(m).start()
    sib_real().start()

    def prepare_half(chunk, which):
        rows = pl.ds(chunk * n_real + which * half, half)
        value = oth[rows, :]
        high, low = split(value)
        oth_high[rows, :] = high
        oth_low[rows, :] = low
        norm = jnp.sum(value * value, axis=1, keepdims=True)
        oth_norm[chunk, :, which * half : (which + 1) * half] = jnp.broadcast_to(norm, (half, 128)).T[0:8, :]

    def prepare_other(chunk):
        prepare_half(chunk, 0)
        prepare_half(chunk, 1)

    def prepare_gen(q):
        rows = tile_rows(q)
        value = gen[rows, :]
        high, low = split(value)
        start = pl.multiple_of(2 * tile * q, tile)
        gen_both[pl.ds(start, tile), :] = high
        gen_both[pl.ds(pl.multiple_of(start + tile, tile), tile), :] = low
        gen_norm[rows, :] = jnp.sum(value * value, axis=1, keepdims=True)

    def tile_rows(q):
        return pl.ds(pl.multiple_of(q * tile, tile), tile)

    def add_pairs(q, chunk, scale):
        rows = tile_rows(q)
        others = pl.ds(pl.multiple_of(chunk * n_real, n_real), n_real)
        start = pl.multiple_of(2 * tile * q, tile)
        inner = product(
            gen_both[pl.ds(start, 2 * tile), :], gen_both[pl.ds(start, tile), :],
            oth_high[others, :], oth_low[others, :], ((1,), (1,)),
        )
        dist = jnp.maximum(gen_norm[rows, :] + oth_norm[chunk, 0:1, :] - 2.0 * inner, 0.0)
        wide = jnp.exp(dist * (-1.0 / (4.0 * width)))
        middle = wide * wide
        weight = (2.0 * (middle * middle) + middle + 0.5 * wide) * scale
        total[rows, :] += jnp.sum(weight, axis=1, keepdims=True)
        w_high, w_low = split(weight)
        w_both = jnp.concatenate([w_high, w_low], axis=0)
        step = 256
        for column in range(0, width, step):
            columns = pl.ds(column, step)
            acc[rows, columns] += product(
                w_both, w_high, oth_high[others, columns], oth_low[others, columns], ((1,), (0,))
            )

    self_scale, cross_scale = 1.0 / total_gen, -1.0 / total_real

    def take_far(m):
        far_real(m).wait_recv()
        forward_real(m).start()

    def take_z(dz):
        z_copy(reps - dz).wait_recv()
        for dh in range(1, his):
            hi_copy(dh, dz, gen.at[block(0, dz)]).start()

    def work(q, first, last):
        def chunk_pairs(chunk, carry):
            add_pairs(q, chunk, jnp.where(chunk == 2, self_scale, cross_scale))
            return carry

        lax.fori_loop(first, last, chunk_pairs, 0)

    def begin(q):
        prepare_gen(q)
        rows = tile_rows(q)
        acc[rows, :] = jnp.zeros((tile, width), jnp.float32)
        total[rows, :] = jnp.zeros((tile, 1), jnp.float32)

    def finish(q):
        rows = tile_rows(q)
        acc[rows, :] = total[rows, :] * gen[rows, :] - acc[rows, :]

    def loop(first, last, step):
        def body(i, carry):
            step(i)
            return carry

        lax.fori_loop(first, last, body, 0)

    prepare_other(0)
    z_copy(1).wait_send()
    z_copy(3).start()
    z_copy(2).start()
    take_z(1)
    far_real(2).start()
    sib_real().wait_recv()
    prepare_other(1)

    def stage_1(dh):
        @pl.when(dh >= 1)
        def _():
            for dz in ORDER[:2]:
                hi_copy(his - dh, dz, own).wait_recv()

        begin(2 * dh)
        work(2 * dh, 0, 2)

    loop(0, his, stage_1)
    take_z(3)
    far_real(3).start()
    far_gen().wait_recv()
    forward_gen().start()
    for m in range(2):
        take_far(m)
    sib_gen().wait_recv()
    forward_gen().wait_recv()
    prepare_other(2)
    for m in range(2):
        forward_real(m).wait_recv()
    prepare_other(3)
    take_z(2)
    loop(0, his, lambda dh: work(2 * dh, 2, 4))
    begin(1)
    work(1, 0, 4)
    for m in range(2, PIECES):
        take_far(m)
    prepare_half(4, 0)
    for m in range(2, PIECES):
        forward_real(m).wait_recv()
    prepare_half(4, 1)

    def stage_3(dh):
        work(2 * dh, 4, 5)
        finish(2 * dh)
        for p in range(PARTS):
            red_hi(dh, 1, p).start()

    def stage_4(dh):
        for dz in ORDER[2:]:
            hi_copy(his - dh, dz, own).wait_recv()
        begin(2 * dh + 1)
        work(2 * dh + 1, 0, 5)
        finish(2 * dh + 1)

    def stage_5(q):
        work(q, 4, 5)
        finish(q)

    loop(1, his, stage_3)
    loop(1, his, stage_4)
    sends = [(dz, p) for dz in (1, 2, 3, 0) for p in range(PARTS)]

    def next_send(i):
        for dh in range(1, his):
            red_hi(dh, *sends[i]).wait_send()
            red_hi(dh, *sends[i + 2]).start()

    next_send(0)
    next_send(1)
    loop(0, 2, stage_5)

    for i, (dz, p) in enumerate(sends):
        rows = part_of(0, dz, p)
        value = acc[rows, :]
        for dh in range(1, his):
            red_hi(his - dh, dz, p).wait_recv()
            value = value + from_hi[dh, dz, pl.ds(p * n_part, n_part), :]
        acc[rows, :] = value
        if dz > 0:
            red_z(dz, p).start()
        if i + 4 < len(sends):
            next_send(i + 2)
    for p in range(PARTS):
        result = acc[part_of(0, 0, p), :]
        for dz in (1, 2, 3):
            red_z(reps - dz, p).wait_recv()
            result = result + from_z[dz, pl.ds(p * n_part, n_part), :]
        out_ref[pl.ds(p * n_part, n_part), :] = result

    sent = [far_gen(), sib_gen(), sib_real(), forward_gen(), z_copy(2), z_copy(3)]
    sent += [far_real(m) for m in range(PIECES)] + [forward_real(m) for m in range(PIECES)]
    sent += [hi_copy(dh, dz, own) for dh in range(1, his) for dz in range(reps)]
    sent += [red_hi(dh, 0, p) for dh in range(1, his) for p in range(PARTS)]
    sent += [red_z(dz, p) for dz in range(1, reps) for p in range(PARTS)]
    for copy in sent:
        copy.wait_send()


def solution(mesh):
    blks, reps = mesh.shape["blk"], mesh.shape["rep"]
    his = blks // GROUP

    def on_device(generated, real_bank, subset_rows):
        n_gen, width = generated.shape
        n_real = subset_rows.shape[0]
        n_other = 5 * n_real
        n_rows = his * reps * n_gen
        dma = pltpu.SemaphoreType.DMA
        vmem = pl.BlockSpec(memory_space=pltpu.VMEM)
        pairs = n_rows * n_other
        return pl.pallas_call(
            functools.partial(kernel, (blks, reps)),
            out_shape=jax.ShapeDtypeStruct((n_gen, width), jnp.float32),
            in_specs=[pl.BlockSpec(memory_space=pltpu.SMEM)] + [pl.BlockSpec(memory_space=pl.ANY)] * 2,
            out_specs=vmem,
            scratch_shapes=[
                pltpu.VMEM(real_bank.shape, jnp.float32),
                dma((3,)),
                pltpu.VMEM((n_other, width), jnp.float32),
                pltpu.VMEM((n_other, width), jnp.bfloat16),
                pltpu.VMEM((n_other, width), jnp.bfloat16),
                pltpu.VMEM((5, 8, n_real), jnp.float32),
                pltpu.VMEM((n_rows, width), jnp.float32),
                pltpu.VMEM((2 * n_rows, width), jnp.bfloat16),
                pltpu.VMEM((n_rows, 1), jnp.float32),
                pltpu.VMEM((n_rows, width), jnp.float32),
                pltpu.VMEM((n_rows, 1), jnp.float32),
                pltpu.VMEM((his, reps, n_gen, width), jnp.float32),
                pltpu.VMEM((reps, n_gen, width), jnp.float32),
                dma((2,)), dma((2,)),
                dma((1 + PIECES,)), dma((1 + PIECES,)),
                dma((1 + PIECES,)), dma((1 + PIECES,)),
                dma((reps,)), dma((reps,)),
                dma((his, reps)), dma((his, reps)),
                dma((his, reps, PARTS)), dma((his, reps, PARTS)),
                dma((reps, PARTS)), dma((reps, PARTS)),
            ],
            compiler_params=pltpu.CompilerParams(
                collective_id=0, has_side_effects=True, vmem_limit_bytes=60 * 1024 * 1024
            ),
            cost_estimate=pl.CostEstimate(
                flops=12 * pairs * width, bytes_accessed=4 * 1024 * width, transcendentals=pairs
            ),
        )(subset_rows, generated, real_bank)

    in_specs = (P(("blk", "rep"), None), P(("blk", "rep"), None), P(("blk", "rep")))
    return jax.shard_map(
        on_device, mesh=mesh, in_specs=in_specs, out_specs=P(("blk", "rep"), None), check_vma=False
    )
```

```python
import functools

import jax
import jax.numpy as jnp
from jax import lax
from jax.experimental import pallas as pl
from jax.experimental.pallas import tpu as pltpu
from jax.sharding import PartitionSpec as P

MESH = pl.DeviceIdType.MESH
GROUP = 4
ORDER = (0, 1, 3, 2)
PARTS = 2
PIECES = 4


def split(value):
    high = value.astype(jnp.bfloat16)
    return high, (value - high.astype(jnp.float32)).astype(jnp.bfloat16)


def dot(a, b, contract):
    return lax.dot_general(a, b, (contract, ((), ())), preferred_element_type=jnp.float32)


def product(a_both, a_high, b_high, b_low, contract):
    rows = a_high.shape[0]
    both = dot(a_both, b_high, contract)
    return both[:rows] + (both[rows:] + dot(a_high, b_low, contract))


def kernel(
    sizes,
    rows_ref, gen_ref, bank_ref, out_ref, bank, load_sem,
    oth, oth_high, oth_low, oth_norm,
    gen, gen_both, gen_norm, acc, total, from_hi, from_z,
    sib_send, sib_recv, far_send, far_recv, fwd_send, fwd_recv,
    z_send, z_recv, hi_send, hi_recv, red_hi_send, red_hi_recv, red_z_send, red_z_recv,
):
    blks, reps = sizes
    his = blks // GROUP
    n_gen, width = gen_ref.shape
    n_real = rows_ref.shape[0]
    piece = n_real // PIECES
    total_gen = n_gen * blks * reps
    total_real = n_real * blks * reps
    assert reps == len(ORDER)
    tile = 2 * n_gen

    blk, rep = lax.axis_index("blk"), lax.axis_index("rep")
    hi, lo = blk // GROUP, lax.rem(blk, GROUP)
    core, side = lax.rem(lo, 2), lo // 2
    sibling = (hi * GROUP + side * 2 + (1 - core), rep)
    across = (hi * GROUP + (1 - side) * 2 + core, rep)

    def z_partner(dz):
        return (blk, lax.rem(rep + dz, reps))

    def hi_partner(dh):
        return (lax.rem(hi + dh, his) * GROUP + lo, rep)

    half = n_real // 2
    c_gen, c_far = 2 * n_real, 3 * n_real

    def far_rows(m, forwarded):
        chunk, part = divmod(m, PIECES // 2)
        return pl.ds(c_far + chunk * n_real + (half if forwarded else 0) + part * piece, piece)

    def gen_rows(slot):
        return pl.ds(c_gen + slot * n_gen, n_gen)

    def block(dh, dz):
        return pl.ds(pl.multiple_of((dh * reps + ORDER.index(dz)) * n_gen, n_gen), n_gen)

    own = gen.at[block(0, 0)]

    def remote(src, dst, send, recv, device):
        return pltpu.make_async_remote_copy(
            src_ref=src, dst_ref=dst, send_sem=send, recv_sem=recv, device_id=device, device_id_type=MESH
        )

    def z_copy(dz):
        back = reps - dz
        return remote(own, gen.at[block(0, back)], z_send.at[dz], z_recv.at[back], z_partner(dz))

    def hi_copy(dh, dz, src):
        back = his - dh
        return remote(src, gen.at[block(back, dz)], hi_send.at[dh, dz], hi_recv.at[back, dz], hi_partner(dh))

    def far_gen():
        return remote(own, oth.at[gen_rows(2)], far_send.at[0], far_recv.at[0], across)

    def far_real(m):
        return remote(
            oth.at[pl.ds(m * piece, piece)], oth.at[far_rows(m, False)],
            far_send.at[1 + m], far_recv.at[1 + m], across,
        )

    def sib_gen():
        return remote(own, oth.at[gen_rows(1)], sib_send.at[0], sib_recv.at[0], sibling)

    def sib_real():
        return remote(
            oth.at[pl.ds(0, n_real)], oth.at[pl.ds(n_real, n_real)], sib_send.at[1], sib_recv.at[1], sibling
        )

    def forward_gen():
        return remote(oth.at[gen_rows(2)], oth.at[gen_rows(3)], fwd_send.at[0], fwd_recv.at[0], sibling)

    def forward_real(m):
        return remote(
            oth.at[far_rows(m, False)], oth.at[far_rows(m, True)],
            fwd_send.at[1 + m], fwd_recv.at[1 + m], sibling,
        )

    n_part = n_gen // PARTS

    def part_of(dh, dz, p):
        start = (dh * reps + ORDER.index(dz)) * n_gen + p * n_part
        return pl.ds(pl.multiple_of(start, n_part), n_part)

    def red_hi(dh, dz, p):
        back = his - dh
        return remote(
            acc.at[part_of(dh, dz, p)], from_hi.at[back, dz, pl.ds(p * n_part, n_part)],
            red_hi_send.at[dh, dz, p], red_hi_recv.at[back, dz, p], hi_partner(dh),
        )

    def red_z(dz, p):
        back = reps - dz
        return remote(
            acc.at[part_of(0, dz, p)], from_z.at[back, pl.ds(p * n_part, n_part)],
            red_z_send.at[dz, p], red_z_recv.at[back, p], z_partner(dz),
        )

    loads = [
        pltpu.make_async_copy(bank_ref, bank, load_sem.at[0]),
        pltpu.make_async_copy(gen_ref, own, load_sem.at[1]),
        pltpu.make_async_copy(gen_ref, oth.at[gen_rows(0)], load_sem.at[2]),
    ]
    for load in loads:
        load.start()
    partners = [sibling, across]
    partners += [z_partner(dz) for dz in range(1, reps)]
    partners += [hi_partner(dh) for dh in range(1, his)]
    barrier = pltpu.get_barrier_semaphore()
    for device in partners:
        pl.semaphore_signal(barrier, inc=1, device_id=device, device_id_type=MESH)
    for load in loads:
        load.wait()

    def gather(i, carry):
        picked = [bank[pl.ds(rows_ref[i * 8 + k], 1), :] for k in range(8)]
        for k in range(8):
            p = i * 8 + k
            oth[pl.ds(p, 1), :] = picked[k]
        return carry

    lax.fori_loop(0, piece // 8, gather, 0)
    pl.semaphore_wait(barrier, len(partners))

    far_gen().start()
    z_copy(1).start()
    for dh in range(1, his):
        hi_copy(dh, 0, own).start()
    far_real(0).start()
    sib_gen().start()
    for m in range(1, PIECES):
        lax.fori_loop(m * piece // 8, (m + 1) * piece // 8, gather, 0)
        if m == 1:
            far_real(m).start()
    sib_real().start()

    def prepare_half(chunk, which):
        rows = pl.ds(chunk * n_real + which * half, half)
        value = oth[rows, :]
        high, low = split(value)
        oth_high[rows, :] = high
        oth_low[rows, :] = low
        norm = jnp.sum(value * value, axis=1, keepdims=True)
        oth_norm[chunk, :, which * half : (which + 1) * half] = jnp.broadcast_to(norm, (half, 128)).T[0:8, :]

    def prepare_other(chunk):
        prepare_half(chunk, 0)
        prepare_half(chunk, 1)

    def prepare_gen(q):
        rows = tile_rows(q)
        value = gen[rows, :]
        high, low = split(value)
        start = pl.multiple_of(2 * tile * q, tile)
        gen_both[pl.ds(start, tile), :] = high
        gen_both[pl.ds(pl.multiple_of(start + tile, tile), tile), :] = low
        gen_norm[rows, :] = jnp.sum(value * value, axis=1, keepdims=True)

    def tile_rows(q):
        return pl.ds(pl.multiple_of(q * tile, tile), tile)

    def add_pairs(q, chunk, scale):
        rows = tile_rows(q)
        others = pl.ds(pl.multiple_of(chunk * n_real, n_real), n_real)
        start = pl.multiple_of(2 * tile * q, tile)
        inner = product(
            gen_both[pl.ds(start, 2 * tile), :], gen_both[pl.ds(start, tile), :],
            oth_high[others, :], oth_low[others, :], ((1,), (1,)),
        )
        dist = jnp.maximum(gen_norm[rows, :] + oth_norm[chunk, 0:1, :] - 2.0 * inner, 0.0)
        wide = jnp.exp(dist * (-1.0 / (4.0 * width)))
        middle = wide * wide
        weight = (2.0 * (middle * middle) + middle + 0.5 * wide) * scale
        total[rows, :] += jnp.sum(weight, axis=1, keepdims=True)
        w_high, w_low = split(weight)
        w_both = jnp.concatenate([w_high, w_low], axis=0)
        step = 256
        for column in range(0, width, step):
            columns = pl.ds(column, step)
            acc[rows, columns] += product(
                w_both, w_high, oth_high[others, columns], oth_low[others, columns], ((1,), (0,))
            )

    self_scale, cross_scale = 1.0 / total_gen, -1.0 / total_real

    def take_far(m):
        far_real(m).wait_recv()
        forward_real(m).start()

    def take_z(dz):
        z_copy(reps - dz).wait_recv()
        for dh in range(1, his):
            hi_copy(dh, dz, gen.at[block(0, dz)]).start()

    def work(q, first, last):
        def chunk_pairs(chunk, carry):
            add_pairs(q, chunk, jnp.where(chunk == 2, self_scale, cross_scale))
            return carry

        lax.fori_loop(first, last, chunk_pairs, 0)

    def begin(q):
        prepare_gen(q)
        rows = tile_rows(q)
        acc[rows, :] = jnp.zeros((tile, width), jnp.float32)
        total[rows, :] = jnp.zeros((tile, 1), jnp.float32)

    def finish(q):
        rows = tile_rows(q)
        acc[rows, :] = total[rows, :] * gen[rows, :] - acc[rows, :]

    def loop(first, last, step):
        def body(i, carry):
            step(i)
            return carry

        lax.fori_loop(first, last, body, 0)

    prepare_other(0)
    z_copy(1).wait_send()
    z_copy(3).start()
    z_copy(2).start()
    take_z(1)
    far_real(2).start()
    sib_real().wait_recv()
    prepare_other(1)

    def stage_1(dh):
        @pl.when(dh >= 1)
        def _():
            for dz in ORDER[:2]:
                hi_copy(his - dh, dz, own).wait_recv()

        begin(2 * dh)
        work(2 * dh, 0, 2)

    loop(0, his, stage_1)
    take_z(3)
    far_real(3).start()
    far_gen().wait_recv()
    forward_gen().start()
    for m in range(2):
        take_far(m)
    sib_gen().wait_recv()
    forward_gen().wait_recv()
    prepare_other(2)
    for m in range(2):
        forward_real(m).wait_recv()
    prepare_other(3)
    take_z(2)
    loop(0, his, lambda dh: work(2 * dh, 2, 4))
    begin(1)
    work(1, 0, 2)
    take_far(2)
    work(1, 2, 4)
    take_far(3)
    prepare_half(4, 0)
    for m in range(2, PIECES):
        forward_real(m).wait_recv()
    prepare_half(4, 1)

    def stage_3(dh):
        work(2 * dh, 4, 5)
        finish(2 * dh)
        for p in range(PARTS):
            red_hi(dh, 1, p).start()

    def stage_4(dh):
        for dz in ORDER[2:]:
            hi_copy(his - dh, dz, own).wait_recv()
        begin(2 * dh + 1)
        work(2 * dh + 1, 0, 5)
        finish(2 * dh + 1)

    def stage_5(q):
        work(q, 4, 5)
        finish(q)

    loop(1, his, stage_3)
    loop(1, his, stage_4)
    sends = [(dz, p) for dz in (1, 2, 3, 0) for p in range(PARTS)]

    def next_send(i):
        for dh in range(1, his):
            red_hi(dh, *sends[i]).wait_send()
            red_hi(dh, *sends[i + 2]).start()

    next_send(0)
    next_send(1)
    loop(0, 2, stage_5)

    for i, (dz, p) in enumerate(sends):
        rows = part_of(0, dz, p)
        value = acc[rows, :]
        for dh in range(1, his):
            red_hi(his - dh, dz, p).wait_recv()
            value = value + from_hi[dh, dz, pl.ds(p * n_part, n_part), :]
        acc[rows, :] = value
        if dz > 0:
            red_z(dz, p).start()
        if i + 4 < len(sends):
            next_send(i + 2)
    for p in range(PARTS):
        result = acc[part_of(0, 0, p), :]
        for dz in (1, 2, 3):
            red_z(reps - dz, p).wait_recv()
            result = result + from_z[dz, pl.ds(p * n_part, n_part), :]
        out_ref[pl.ds(p * n_part, n_part), :] = result

    sent = [far_gen(), sib_gen(), sib_real(), forward_gen(), z_copy(2), z_copy(3)]
    sent += [far_real(m) for m in range(PIECES)] + [forward_real(m) for m in range(PIECES)]
    sent += [hi_copy(dh, dz, own) for dh in range(1, his) for dz in range(reps)]
    sent += [red_hi(dh, 0, p) for dh in range(1, his) for p in range(PARTS)]
    sent += [red_z(dz, p) for dz in range(1, reps) for p in range(PARTS)]
    for copy in sent:
        copy.wait_send()


def solution(mesh):
    blks, reps = mesh.shape["blk"], mesh.shape["rep"]
    his = blks // GROUP

    def on_device(generated, real_bank, subset_rows):
        n_gen, width = generated.shape
        n_real = subset_rows.shape[0]
        n_other = 5 * n_real
        n_rows = his * reps * n_gen
        dma = pltpu.SemaphoreType.DMA
        vmem = pl.BlockSpec(memory_space=pltpu.VMEM)
        pairs = n_rows * n_other
        return pl.pallas_call(
            functools.partial(kernel, (blks, reps)),
            out_shape=jax.ShapeDtypeStruct((n_gen, width), jnp.float32),
            in_specs=[pl.BlockSpec(memory_space=pltpu.SMEM)] + [pl.BlockSpec(memory_space=pl.ANY)] * 2,
            out_specs=vmem,
            scratch_shapes=[
                pltpu.VMEM(real_bank.shape, jnp.float32),
                dma((3,)),
                pltpu.VMEM((n_other, width), jnp.float32),
                pltpu.VMEM((n_other, width), jnp.bfloat16),
                pltpu.VMEM((n_other, width), jnp.bfloat16),
                pltpu.VMEM((5, 8, n_real), jnp.float32),
                pltpu.VMEM((n_rows, width), jnp.float32),
                pltpu.VMEM((2 * n_rows, width), jnp.bfloat16),
                pltpu.VMEM((n_rows, 1), jnp.float32),
                pltpu.VMEM((n_rows, width), jnp.float32),
                pltpu.VMEM((n_rows, 1), jnp.float32),
                pltpu.VMEM((his, reps, n_gen, width), jnp.float32),
                pltpu.VMEM((reps, n_gen, width), jnp.float32),
                dma((2,)), dma((2,)),
                dma((1 + PIECES,)), dma((1 + PIECES,)),
                dma((1 + PIECES,)), dma((1 + PIECES,)),
                dma((reps,)), dma((reps,)),
                dma((his, reps)), dma((his, reps)),
                dma((his, reps, PARTS)), dma((his, reps, PARTS)),
                dma((reps, PARTS)), dma((reps, PARTS)),
            ],
            compiler_params=pltpu.CompilerParams(
                collective_id=0, has_side_effects=True, vmem_limit_bytes=60 * 1024 * 1024
            ),
            cost_estimate=pl.CostEstimate(
                flops=12 * pairs * width, bytes_accessed=4 * 1024 * width, transcendentals=pairs
            ),
        )(subset_rows, generated, real_bank)

    in_specs = (P(("blk", "rep"), None), P(("blk", "rep"), None), P(("blk", "rep")))
    return jax.shard_map(
        on_device, mesh=mesh, in_specs=in_specs, out_specs=P(("blk", "rep"), None), check_vma=False
    )
```
